512 devices in a mesh: row: 128 (over y, z, core), col: 4 (over x).
Axes of the slice: x: 4, y: 4, z: 16, core: 2. Of those that a mesh axis runs over, the one named last changes fastest.
Arguments:
- activations: float32 [4, 256, 6144], P(None, 'row', 'col'), may hold values from -500 to 500
- input_weight: float32 [3, 32, 128, 6144], P(None, None, 'row', 'col'), may hold values from -0.078125 to 0.078125
- output_weight: float32 [6144, 32, 128], P('row', 'col'), may hold values from -0.5 to 0.5
Outputs:
- block_output: float32 [4, 256, 6144], P(None, 'col', 'row')
The draws below stay inside these ranges and needn't reach their ends.
All inputs are finite; a program needn't handle non-finite values.
Results may differ from the reference program's by a relative error of at most 0.00013.
Values sent between devices are 32-bit elements; how exact they have to be, the bound alone decides.
A program may use at most 64 MiB of HBM per device.

```python
import math
import jax
import jax.numpy as jnp
from jax import lax

D = 6144
H = 32
DH = 128
PATCH = 256
IMG = 4


def draw_activations(key, part):
    key = jax.random.fold_in(key, 7)
    subkeys = jax.random.split(key, 3)
    baseline = jax.random.normal(subkeys[0], (IMG, PATCH, D), jnp.float32)
    baseline = jnp.clip(baseline, -5.0, 5.0)
    row_scale = jnp.exp(jax.random.uniform(subkeys[1], (IMG, PATCH, 1), jnp.float32, 0.0, math.log(10.0)))
    col_scale = jnp.exp(jax.random.uniform(subkeys[2], (1, 1, D), jnp.float32, 0.0, math.log(10.0)))
    return (baseline * row_scale * col_scale).astype(jnp.float32)


def steps_of(rng, shape, cuts, least, high):
    loudness = 1.0
    for position, parts in cuts:
        steps = jax.random.uniform(jax.random.fold_in(jax.random.fold_in(rng, 6), position), (parts,), jnp.float32, least / len(cuts), high / len(cuts))
        loudness = loudness * jnp.repeat(jnp.exp(steps), shape[position] // parts).reshape((-1,) + (1,) * (len(shape) - 1 - position))
    return loudness


def scatter_about(rng, shape, width, reach, pieces=(), held_as=jnp.bfloat16):
    drawn = jax.random.normal(rng, shape, jnp.float32) * width
    if len(pieces) > 0:
        drawn = steps_of(rng, shape, pieces, -0.22, 0.18) * drawn
    return jnp.clip(drawn, min=-reach, max=reach).astype(held_as)


def setup_inputs(seed: int = 0) -> dict:
    streams_of = jax.random.split(jax.random.key(seed), 4)
    activations = draw_activations(jax.random.fold_in(streams_of[3], 71), 0)
    input_weight = scatter_about(streams_of[1], (3, H, DH, D), D ** -0.5, 0.078125, ((2, 128), (3, 4)), jnp.float32)
    output_weight = scatter_about(streams_of[2], (D, H, DH), DH ** -0.5, 0.5, ((0, 128), (1, 4)), jnp.float32)
    return {"activations": activations, "input_weight": input_weight, "output_weight": output_weight}


epsilon = 1e-06
highest = lax.Precision.HIGHEST

def layer_norm(values):
    center = lax.optimization_barrier(jnp.mean(values, -1, keepdims=True))
    spread = lax.optimization_barrier(jnp.mean(values * values, -1, keepdims=True)) - center * center
    return (values - center) * lax.rsqrt(spread + epsilon)

def reference(activations, input_weight, output_weight):
    normed = layer_norm(activations)
    triples = jnp.einsum('ipe,shde->ipshd', normed, input_weight, precision=highest)
    queries = layer_norm(triples[:, :, 0])
    keys = layer_norm(triples[:, :, 1])
    values = triples[:, :, 2]
    scores = jnp.einsum('iqhd,ikhd->ihqk', queries, keys, precision=highest) * DH ** (-0.5)
    weights = jnp.exp(scores)
    weights = weights / lax.optimization_barrier(jnp.sum(weights, -1, keepdims=True))
    attended = jnp.einsum('ihqk,ikhd->iqhd', weights, values, precision=highest)
    return jnp.einsum('iqhd,nhd->iqn', attended, output_weight, precision=highest)
```

```python
import jax
import jax.numpy as jnp
from jax import lax
from jax.experimental import pallas as pl
from jax.experimental.pallas import tpu as pltpu
from jax.sharding import PartitionSpec as P

MESH = pl.DeviceIdType.MESH
EPS = 1e-06
HIGHEST = lax.Precision.HIGHEST
F32 = jnp.float32
BF16 = jnp.bfloat16

NX, NY, NZ, NC = 4, 4, 16, 2
LANE = 128
TILES = 48
KT = TILES // NX
R1, R2 = 64, 32
HEADS = 32
NZZ = 8
A1 = 80
FEAT = 96
NOUT = 48


def split(x):
    hi = x.astype(BF16)
    return hi, (x - hi.astype(F32)).astype(BF16)


def kernel(act, w, ow, out, *scratch):
    (chunk, g1, g2, wb, whl, ghl, ob, owhl, msg, rcv, kv, att, fs, fr, acc,
     act_s, act_r, w_s, w_r, wf_s, wf_r, wc_s, wc_r, o_s, o_r, of_s, of_r, oc_s, oc_r,
     s1, r1, s2, r2, sy, ry, syh, ryh, sp, rp, a2a_s, a2a_r, kv_s, kv_r,
     t1, u1, t2, u2, ty, uy, tyh, uyh, tp, up, f_s, f_r, loc) = scratch
    row = lax.axis_index("row")
    x = lax.axis_index("col")
    c = row % 2
    z = row // 2 % NZ
    y = row // (2 * NZ)
    oc = 1 - c

    def dev(yy, zz, cc, xx):
        return ((yy * NZ + zz) * 2 + cc, xx)

    def wrap(v, n):
        return (v + n) % n

    def remote(src, dst, ssem, rsem, where):
        copy = pltpu.make_async_remote_copy(
            src_ref=src, dst_ref=dst, send_sem=ssem, recv_sem=rsem, device_id=where, device_id_type=MESH
        )
        copy.start()

    def wait(ref, sem):
        pltpu.make_async_copy(ref, ref, sem).wait()

    xp, xm, xo = wrap(x + 1, NX), wrap(x - 1, NX), wrap(x + 2, NX)
    yp, ym, yo = wrap(y + 1, NY), wrap(y - 1, NY), wrap(y + 2, NY)
    zp, zm = wrap(z + 1, NZ), wrap(z - 1, NZ)

    bar = pltpu.get_barrier_semaphore()
    me = y * NZ + z

    def greet(k, carry):
        other = (me + k) % (NY * NZ)
        pl.semaphore_signal(bar, inc=1, device_id=(other * 2 + c, x), device_id_type=MESH)
        return carry

    lax.fori_loop(1, NY * NZ, greet, 0)
    for dx in range(NX):
        for dc in range(NC):
            if dx or dc:
                pl.semaphore_signal(
                    bar, inc=1, device_id=dev(y, z, (c + dc) % 2, (x + dx) % NX), device_id_type=MESH
                )
    pl.semaphore_wait(bar, NY * NZ - 1 + NX * NC - 1)

    for i in range(1, NX):
        xt = (x + i) % NX
        remote(act.at[xt], chunk.at[x], act_s.at[i], act_r.at[i], dev(y, z, c, xt))

    def gather_start(src, buf, half, ss, rs, cs, cr, ls):
        for q, (first, target) in enumerate(((0, xp), (1, xm))):
            for p in (first, 1 - first):
                rows = pl.ds(p * half, half)
                remote(src.at[rows], buf.at[c, x, rows], ss.at[q, p], rs.at[q, p], dev(y, z, c, target))
        for p in range(2):
            rows = pl.ds(p * half, half)
            remote(src.at[rows], buf.at[c, x, rows], cs.at[p], cr.at[p], dev(y, z, oc, x))
        pltpu.make_async_copy(src, buf.at[c, x], ls).start()

    def gather_pass(buf, half, q, p, ss, rs, fs_, fr_, cs, cr):
        origin = xm if q == 0 else xp
        rows = pl.ds(p * half, half)
        piece = buf.at[c, origin, rows]
        wait(piece, rs.at[q, p])
        if p == q:
            remote(piece, piece, fs_.at[q], fr_.at[q], dev(y, z, c, xp if q == 0 else xm))
        remote(piece, piece, cs.at[2 + 2 * q + p], cr.at[2 + 2 * q + p], dev(y, z, oc, x))

    def gather_last(buf, half, fr_, cs, cr):
        for q in range(2):
            rows = pl.ds(q * half, half)
            piece = buf.at[c, xo, rows]
            wait(piece, fr_.at[q])
            remote(piece, piece, cs.at[6 + q], cr.at[6 + q], dev(y, z, oc, x))

    def gather_core(buf, half, cr):
        for k, origin in enumerate((x, xm, xp, xo)):
            for p in range(2):
                wait(buf.at[oc, origin, pl.ds(p * half, half)], cr.at[2 * k + p])

    def gather_drain(src, buf, half, ss, fs_, cs):
        for q in range(2):
            for p in range(2):
                wait(src.at[pl.ds(p * half, half)], ss.at[q, p])
            wait(src.at[pl.ds(0, half)], fs_.at[q])
        for k in range(8):
            wait(src.at[pl.ds(0, half)], cs.at[k])

    WH = FEAT * KT // 2
    OH = NOUT * 8 // 2
    gather_start(w, wb, WH, w_s, w_r, wc_s, wc_r, loc.at[0])

    chunk[x] = act[x]
    for i in range(1, NX):
        wait(chunk.at[0], act_r.at[i])
    data = chunk[...].reshape(2 * TILES, LANE)
    odd = lax.broadcasted_iota(jnp.int32, (2 * TILES, LANE), 0) % 2 == 1
    square = data * data
    zero = jnp.zeros_like(data)

    def total(v):
        return jnp.sum(jnp.sum(v, 0, keepdims=True), 1, keepdims=True)

    width = TILES * LANE
    center = [total(jnp.where(odd, data, zero) if b else jnp.where(odd, zero, data)) / width for b in range(2)]
    second = [total(jnp.where(odd, square, zero) if b else jnp.where(odd, zero, square)) / width for b in range(2)]
    scale = [lax.rsqrt(second[b] - center[b] * center[b] + EPS) for b in range(2)]
    normed = (data - jnp.where(odd, center[1], center[0])) * jnp.where(odd, scale[1], scale[0])
    g1[y, z] = normed[:R1]
    g2[y, z] = normed[R1:]

    def z1(d, s, half=False):
        slot = wrap(z - (s - 1), NZ) if d == 0 else wrap(z + (s - 1), NZ)
        piece = g1.at[y, slot, pl.ds(d * (R1 // 2), R1 // 2)] if half else g1.at[y, slot]
        remote(piece, piece, s1.at[d, s - 1], r1.at[d, s - 1], dev(y, zp if d == 0 else zm, c, x))

    def z2(d, s, half=False):
        slot = wrap(z - (s - 1), NZ) if d == 0 else wrap(z + (s - 1), NZ)
        piece = g2.at[:, slot, pl.ds(d * (R2 // 2), R2 // 2)] if half else g2.at[:, slot]
        remote(piece, piece, s2.at[d, s - 1], r2.at[d, s - 1], dev(y, zp if d == 0 else zm, c, x))

    def y1(slot):
        piece = g1.at[y, slot]
        remote(piece, piece, sy.at[0, slot], ry.at[0, slot], dev(yp, z, c, x))
        remote(piece, piece, sy.at[1, slot], ry.at[1, slot], dev(ym, z, c, x))

    def y1pass(slot):
        wait(g1.at[ym, slot], ry.at[0, slot])
        piece = g1.at[ym, slot, pl.ds(0, R1 // 2)]
        remote(piece, piece, syh.at[0, slot], ryh.at[0, slot], dev(yp, z, c, x))
        wait(g1.at[yp, slot], ry.at[1, slot])
        piece = g1.at[yp, slot, pl.ds(R1 // 2, R1 // 2)]
        remote(piece, piece, syh.at[1, slot], ryh.at[1, slot], dev(ym, z, c, x))

    z1(0, 1)
    z1(1, 1)
    own2 = g2.at[y, z]
    for k, target in enumerate((yp, ym, yo)):
        remote(own2, own2, sp.at[k], rp.at[k], dev(target, z, c, x))
    y1(z)
    for k, origin in enumerate((ym, yp, yo)):
        wait(g2.at[origin, z], rp.at[k])
    z2(0, 1)
    z2(1, 1)

    def step(s, half=False):
        back, ahead = wrap(z - s, NZ), wrap(z + s, NZ)
        wait(g1.at[y, back], r1.at[0, s - 1])
        z1(0, s + 1, half)
        y1(back)
        wait(g1.at[y, ahead], r1.at[1, s - 1])
        z1(1, s + 1, half)
        y1(ahead)
        wait(g2.at[:, back], r2.at[0, s - 1])
        z2(0, s + 1, half)
        wait(g2.at[:, ahead], r2.at[1, s - 1])
        z2(1, s + 1, half)

    def wconv(d2, origin, p):
        def body(kt, carry):
            v = wb[d2, origin, pl.ds(p * WH + kt, FEAT // 2, stride=KT), :]
            hi, lo = split(v)
            lanes = pl.ds(pl.multiple_of(kt * LANE, LANE), LANE)
            at = pl.multiple_of(d2 * FEAT + p * (FEAT // 2), 16)
            whl[origin, pl.ds(at, FEAT // 2), lanes] = hi
            whl[origin, pl.ds(at + 2 * FEAT, FEAT // 2), lanes] = lo
            return carry

        lax.fori_loop(0, KT, body, 0)

    W = (w_s, w_r, wf_s, wf_r, wc_s, wc_r)
    O = (o_s, o_r, of_s, of_r, oc_s, oc_r)
    for s in range(1, 8):
        step(s, s == 7)
        if s == 1:
            y1pass(z)
        else:
            y1pass(wrap(z - (s - 1), NZ))
            y1pass(wrap(z + (s - 1), NZ))
        if s == 1:
            wait(w, loc.at[0])
            for p in range(2):
                wconv(c, x, p)
        if s == 2:
            gather_pass(wb, WH, 0, 0, *W)
            gather_pass(wb, WH, 1, 1, *W)
        if s == 3:
            wconv(c, xm, 0)
            wconv(c, xp, 1)
        if s == 5:
            gather_pass(wb, WH, 0, 1, *W)
            gather_pass(wb, WH, 1, 0, *W)
            gather_start(ow, ob, OH, o_s, o_r, oc_s, oc_r, loc.at[1])
        if s == 6:
            wconv(c, xm, 1)
            wconv(c, xp, 0)
    far = wrap(z + 8, NZ)
    wait(g1.at[y, far, pl.ds(0, R1 // 2)], r1.at[0, 7])
    wait(g1.at[y, far, pl.ds(R1 // 2, R1 // 2)], r1.at[1, 7])
    y1(far)
    y1pass(wrap(z - 7, NZ))
    y1pass(wrap(z + 7, NZ))
    gather_last(wb, WH, wf_r, wc_s, wc_r)
    wait(g2.at[:, far, pl.ds(0, R2 // 2)], r2.at[0, 7])
    wait(g2.at[:, far, pl.ds(R2 // 2, R2 // 2)], r2.at[1, 7])
    y1pass(far)
    for p in range(2):
        wconv(c, xo, p)
    gather_core(wb, WH, wc_r)
    for k in range(NX):
        for p in range(2):
            wconv(oc, k, p)
    gather_pass(ob, OH, 0, 0, *O)
    gather_pass(ob, OH, 1, 1, *O)

    def ywait(slot, carry):
        wait(g1.at[yo, slot, pl.ds(0, R1 // 2)], ryh.at[0, slot])
        wait(g1.at[yo, slot, pl.ds(R1 // 2, R1 // 2)], ryh.at[1, slot])
        return carry

    lax.fori_loop(0, NZ, ywait, 0)

    f1 = g1.reshape(NY * NZ * R1, LANE)
    f2 = g2.reshape(NY * NZ * R2, LANE)
    for t in range(TILES):
        for b in range(2):
            if 2 * t < R1:
                v = f1[pl.ds(2 * t + b, NY * NZ, stride=R1), :]
            else:
                v = f2[pl.ds(2 * t - R1 + b, NY * NZ, stride=R2), :]
            hi, lo = split(v)
            lanes = pl.ds(t % KT * LANE, LANE)
            ghl[t // KT, pl.ds(b * 64, 64), lanes] = hi
            ghl[t // KT, pl.ds(128 + b * 64, 64), lanes] = lo
    acc[...] = jnp.zeros_like(acc)

    def project(k, carry):
        acc[...] += lax.dot_general(
            whl[k], ghl[k], (((1,), (1,)), ((), ())), preferred_element_type=F32
        )
        return carry

    lax.fori_loop(0, NX, project, 0)
    full = acc[...]
    half_sum = full[:, :LANE] + full[:, LANE:]
    triples = half_sum[: 2 * FEAT] + half_sum[2 * FEAT :]

    msg[...] = jnp.zeros_like(msg)
    for d2 in range(2):
        for s in range(3):
            at = d2 * FEAT + s * HEADS
            msg[pl.ds(2 * s + d2, HEADS, stride=8), :] = triples[at : at + HEADS]

    def post(k, carry):
        h = (k + me // 2) % HEADS
        there = h // NZZ * NZ + h % NZZ * 2
        src = msg.at[pl.ds(pl.multiple_of(h * 8, 8), 8)]
        dst = rcv.at[pl.ds(pl.multiple_of(me * 8, 8), 8)]

        @pl.when(there != me)
        def _():
            remote(src, dst, a2a_s, a2a_r, (there * 2 + c, x))

        @pl.when(there == me)
        def _():
            pltpu.make_async_copy(src, dst, a2a_r).start()

        return carry

    lax.fori_loop(0, HEADS, post, 0)

    gather_pass(ob, OH, 0, 1, *O)
    gather_pass(ob, OH, 1, 0, *O)
    gather_last(ob, OH, of_r, oc_s, oc_r)
    wait(ow, loc.at[1])
    gather_core(ob, OH, oc_r)

    for d2 in range(2):
        for hq in range(NX):
            for j in range(8):
                v = ob[d2, hq, pl.ds(j, NOUT, stride=8), :]
                hi, lo = split(v)
                lanes = pl.ds(hq * LANE, LANE)
                owhl[j, pl.ds(d2 * NOUT, NOUT), lanes] = hi
                owhl[j, pl.ds(2 * NOUT + d2 * NOUT, NOUT), lanes] = lo

    even = z % 2 == 0
    zz0 = z // 2

    def norm_rows(v):
        m = jnp.sum(v, 0, keepdims=True) / LANE
        q = jnp.sum(v * v, 0, keepdims=True) / LANE - m * m
        return (v - m) * lax.rsqrt(q + EPS)

    @pl.when(even)
    def _():
        wait(rcv, a2a_r)

        def part(s):
            return jnp.concatenate([rcv[pl.ds(2 * s + d2, 64, stride=8), :] for d2 in range(2)], 0)

        kv[c, pl.ds(0, LANE)] = norm_rows(part(1))
        kv[c, pl.ds(LANE, LANE)] = part(2)
        mine = kv.at[c]
        remote(mine, mine, kv_s, kv_r, dev(y, z, oc, x))
        queries = norm_rows(part(0)) * (LANE ** -0.5)
        wait(kv.at[oc], kv_r)
        es = []
        for k in range(2):
            keys = kv[k, pl.ds(0, LANE)].T
            es.append(jnp.exp(jnp.dot(keys, queries, precision=HIGHEST, preferred_element_type=F32)))
        norm = jnp.sum(es[0], 0, keepdims=True) + jnp.sum(es[1], 0, keepdims=True)
        o = sum(
            jnp.dot(kv[k, pl.ds(LANE, LANE)], es[k] / norm, precision=HIGHEST, preferred_element_type=F32)
            for k in range(2)
        )
        for d2 in range(2):
            att[zz0, y, pl.ds(d2, 64, stride=2), :] = o[d2 * 64 : d2 * 64 + 64]

    A2 = LANE - A1

    def slot_of(d, k):
        return wrap(zz0 - k, NZZ) if d == 0 else wrap((z + 1) // 2 + k, NZZ)

    def b1(d, k, half=False):
        slot = slot_of(d, k)
        rows = pl.ds(d * (A1 // 2), A1 // 2) if half else pl.ds(0, A1)
        piece = att.at[slot, y, rows]
        remote(piece, piece, t1.at[d, k], u1.at[d, k], dev(y, zp if d == 0 else zm, c, x))

    def b2(d, k, half=False):
        slot = slot_of(d, k)
        rows = pl.ds(A1 + d * (A2 // 2), A2 // 2) if half else pl.ds(A1, A2)
        piece = att.at[slot, :, rows]
        remote(piece, piece, t2.at[d, k], u2.at[d, k], dev(y, zp if d == 0 else zm, c, x))

    def v1(slot):
        piece = att.at[slot, y, pl.ds(0, A1)]
        remote(piece, piece, ty.at[0, slot], uy.at[0, slot], dev(yp, z, c, x))
        remote(piece, piece, ty.at[1, slot], uy.at[1, slot], dev(ym, z, c, x))

    def v1pass(slot):
        wait(att.at[slot, ym, pl.ds(0, A1)], uy.at[0, slot])
        piece = att.at[slot, ym, pl.ds(0, A1 // 2)]
        remote(piece, piece, tyh.at[0, slot], uyh.at[0, slot], dev(yp, z, c, x))
        wait(att.at[slot, yp, pl.ds(0, A1)], uy.at[1, slot])
        piece = att.at[slot, yp, pl.ds(A1 // 2, A1 // 2)]
        remote(piece, piece, tyh.at[1, slot], uyh.at[1, slot], dev(ym, z, c, x))

    acc2 = acc.at[pl.ds(0, 4 * NOUT)]
    acc2[...] = jnp.zeros((4 * NOUT, 2 * LANE), F32)

    def finish(slot):
        wait(att.at[slot, yo, pl.ds(0, A1 // 2)], uyh.at[0, slot])
        wait(att.at[slot, yo, pl.ds(A1 // 2, A1 // 2)], uyh.at[1, slot])
        block = att[slot].reshape(NY * LANE, LANE)
        hi, lo = split(block)
        acc2[...] += jnp.dot(owhl[slot], jnp.concatenate([hi, lo], 1), preferred_element_type=F32)

    @pl.when(even)
    def _():
        b1(0, 0)
        b1(1, 0)
        own = att.at[zz0, y, pl.ds(A1, A2)]
        for k, target in enumerate((yp, ym, yo)):
            remote(own, own, tp.at[k], up.at[k], dev(target, z, c, x))
        v1(zz0)
        for k, origin in enumerate((ym, yp, yo)):
            wait(att.at[zz0, origin, pl.ds(A1, A2)], up.at[k])
        b2(0, 0)
        b2(1, 0)
        for k in range(1, 4):
            for d in range(2):
                slot = slot_of(d, k)
                wait(att.at[slot, y, pl.ds(0, A1)], u1.at[d, k - 1])
                b1(d, k)
                v1(slot)
            for d in range(2):
                slot = slot_of(d, k)
                wait(att.at[slot, :, pl.ds(A1, A2)], u2.at[d, k - 1])
                b2(d, k)
            if k == 1:
                v1pass(zz0)
                finish(zz0)
            else:
                for d in range(2):
                    v1pass(slot_of(d, k - 1))
                for d in range(2):
                    finish(slot_of(d, k - 1))
        slot = slot_of(0, 4)
        wait(att.at[slot, y, pl.ds(0, A1 // 2)], u1.at[0, 3])
        wait(att.at[slot, y, pl.ds(A1 // 2, A1 // 2)], u1.at[1, 3])
        v1(slot)
        wait(att.at[slot, :, pl.ds(A1, A2 // 2)], u2.at[0, 3])
        wait(att.at[slot, :, pl.ds(A1 + A2 // 2, A2 // 2)], u2.at[1, 3])
        for d in range(2):
            v1pass(slot_of(d, 3))
        v1pass(slot)
        for d in range(2):
            finish(slot_of(d, 3))
        finish(slot)

    @pl.when(jnp.logical_not(even))
    def _():
        for k in range(4):
            half = k == 3
            for d in range(2):
                slot = slot_of(d, k)
                wait(att.at[slot, y, pl.ds(0, A1)], u1.at[d, k])
                b1(d, k, half)
                v1(slot)
            for d in range(2):
                slot = slot_of(d, k)
                wait(att.at[slot, :, pl.ds(A1, A2)], u2.at[d, k])
                b2(d, k, half)
            if k:
                for d in range(2):
                    v1pass(slot_of(d, k - 1))
                for d in range(2):
                    finish(slot_of(d, k - 1))
        for d in range(2):
            v1pass(slot_of(d, 3))
        for d in range(2):
            finish(slot_of(d, 3))

    sums = acc2[...]
    sums = sums[:, :LANE] + sums[:, LANE:]
    sums = sums[: 2 * NOUT] + sums[2 * NOUT :]
    blocks = jnp.concatenate([sums, jnp.zeros((LANE - 2 * NOUT, LANE), F32)], 0).T
    for q in range(NX):
        for cc in range(NC):
            for b in range(2):
                at = b * 64 + q * 16
                fs[q, cc, pl.ds(b * 16, 16), pl.ds(0, NOUT)] = blocks[at : at + 16, cc * NOUT : cc * NOUT + NOUT]
    for dx in range(NX):
        for dc in range(NC):
            if dx or dc:
                tx, tc = (x + dx) % NX, (c + dc) % 2
                remote(fs.at[tx, tc], fr.at[x, c], f_s.at[dx, dc], f_r.at[dx, dc], dev(y, z, tc, tx))
    fr[x, c] = fs[x, c]
    for dx in range(NX):
        for dc in range(NC):
            if dx or dc:
                wait(fr.at[0, 0], f_r.at[dx, dc])
    for i in range(NX):
        for cc in range(NC):
            for b in range(2):
                out[i, pl.ds(2 * cc + b, 16, stride=4), :] = fr[i, cc, pl.ds(b * 16, 16), pl.ds(0, NOUT)]

    for i in range(1, NX):
        wait(chunk.at[0], act_s.at[i])
    gather_drain(w, wb, WH, w_s, wf_s, wc_s)
    gather_drain(ow, ob, OH, o_s, of_s, oc_s)
    for d in range(2):
        for s in range(8):
            wait(g1.at[0, 0, pl.ds(0, R1 // 2)] if s == 7 else g1.at[0, 0], s1.at[d, s])
            wait(g2.at[:, 0, pl.ds(0, R2 // 2)] if s == 7 else g2.at[:, 0], s2.at[d, s])
    for k in range(3):
        wait(own2, sp.at[k])

    def ydrain(slot, carry):
        for d in range(2):
            wait(g1.at[0, 0], sy.at[d, slot])
            wait(g1.at[0, 0, pl.ds(0, R1 // 2)], syh.at[d, slot])
        return carry

    lax.fori_loop(0, NZ, ydrain, 0)

    def vdrain(slot, carry):
        for d in range(2):
            wait(att.at[0, 0, pl.ds(0, A1)], ty.at[d, slot])
            wait(att.at[0, 0, pl.ds(0, A1 // 2)], tyh.at[d, slot])
        return carry

    lax.fori_loop(0, NZZ, vdrain, 0)
    for d in range(2):
        for k in range(3):
            wait(att.at[0, 0, pl.ds(0, A1)], t1.at[d, k])
            wait(att.at[0, :, pl.ds(A1, A2)], t2.at[d, k])

    @pl.when(even)
    def _():
        wait(msg.at[pl.ds(0, (HEADS - 1) * 8)], a2a_s)
        wait(kv.at[0], kv_s)
        for k in range(3):
            wait(att.at[0, 0, pl.ds(A1, A2)], tp.at[k])
        for d in range(2):
            wait(att.at[0, 0, pl.ds(0, A1)], t1.at[d, 3])
            wait(att.at[0, :, pl.ds(A1, A2)], t2.at[d, 3])

    @pl.when(jnp.logical_not(even))
    def _():
        wait(msg, a2a_s)
        for d in range(2):
            wait(att.at[0, 0, pl.ds(0, A1 // 2)], t1.at[d, 3])
            wait(att.at[0, :, pl.ds(A1, A2 // 2)], t2.at[d, 3])

    for dx in range(NX):
        for dc in range(NC):
            if dx or dc:
                wait(fs.at[0, 0], f_s.at[dx, dc])


def shards(activations, input_weight, output_weight):
    images = activations.shape[0]
    act = activations.reshape(images, 2, KT, LANE).transpose(0, 2, 1, 3).reshape(images, 2 * KT, LANE)
    w = input_weight.reshape(FEAT * KT, LANE)
    ow = output_weight.reshape(NOUT * 8, LANE)
    dma = pltpu.SemaphoreType.DMA
    vm = pltpu.VMEM
    scratch = [
        vm((NX, 2 * KT, LANE), F32),
        vm((NY, NZ, R1, LANE), F32),
        vm((NY, NZ, R2, LANE), F32),
        vm((NC, NX, FEAT * KT, LANE), F32),
        vm((NX, 4 * FEAT, KT * LANE), BF16),
        vm((NX, 2 * LANE, KT * LANE), BF16),
        vm((NC, NX, NOUT * 8, LANE), F32),
        vm((NZZ, 4 * NOUT, NY * LANE), BF16),
        vm((HEADS * 8, LANE), F32),
        vm((NY * NZ * 8, LANE), F32),
        vm((NC, 2 * LANE, LANE), F32),
        vm((NZZ, NY, LANE, LANE), F32),
        vm((NX, NC, 32, LANE), F32),
        vm((NX, NC, 32, LANE), F32),
        vm((4 * FEAT, 2 * LANE), F32),
        dma((NX,)), dma((NX,)),
        dma((2, 2)), dma((2, 2)), dma((2,)), dma((2,)), dma((8,)), dma((8,)),
        dma((2, 2)), dma((2, 2)), dma((2,)), dma((2,)), dma((8,)), dma((8,)),
        dma((2, 8)), dma((2, 8)), dma((2, 8)), dma((2, 8)),
        dma((2, NZ)), dma((2, NZ)), dma((2, NZ)), dma((2, NZ)),
        dma((3,)), dma((3,)),
        dma, dma, dma, dma,
        dma((2, 4)), dma((2, 4)), dma((2, 4)), dma((2, 4)),
        dma((2, NZZ)), dma((2, NZZ)), dma((2, NZZ)), dma((2, NZZ)),
        dma((3,)), dma((3,)),
        dma((NX, NC)), dma((NX, NC)),
        dma((2,)),
    ]
    return pl.pallas_call(
        kernel,
        out_shape=jax.ShapeDtypeStruct((NX, 64, NOUT), F32),
        in_specs=[
            pl.BlockSpec(memory_space=pltpu.VMEM),
            pl.BlockSpec(memory_space=pl.ANY),
            pl.BlockSpec(memory_space=pl.ANY),
        ],
        out_specs=pl.BlockSpec(memory_space=pltpu.VMEM),
        scratch_shapes=scratch,
        compiler_params=pltpu.CompilerParams(
            collective_id=0, has_side_effects=True, vmem_limit_bytes=48 * 1024 * 1024
        ),
    )(act, w, ow)


def solution(mesh):
    return jax.shard_map(
        shards,
        mesh=mesh,
        in_specs=(P(None, "row", "col"), P(None, None, "row", "col"), P("row", "col", None)),
        out_specs=P(None, "col", "row"),
        check_vma=False,
    )
```

```python
import jax
import jax.numpy as jnp
from jax import lax
from jax.experimental import pallas as pl
from jax.experimental.pallas import tpu as pltpu
from jax.sharding import PartitionSpec as P

MESH = pl.DeviceIdType.MESH
EPS = 1e-06
HIGHEST = lax.Precision.HIGHEST
F32 = jnp.float32
BF16 = jnp.bfloat16

NX, NY, NZ, NC = 4, 4, 16, 2
LANE = 128
TILES = 48
KT = TILES // NX
R1, R2 = 64, 32
HEADS = 32
NZZ = 8
A1 = 80
FEAT = 96
NOUT = 48


def split(x):
    hi = x.astype(BF16)
    return hi, (x - hi.astype(F32)).astype(BF16)


def kernel(act, w, ow, out, *scratch):
    (chunk, g1, g2, wb, whl, ghl, ob, owhl, msg, rcv, kv, att, fs, fr, acc,
     act_s, act_r, w_s, w_r, wf_r, wc_s, wc_r, o_s, o_r, of_r, oc_s, oc_r,
     z1_s, z2_s, y_s, h_s, c_s, p_s, r1, r2, ry, rh, rp, rc1, rc2,
     a2a_s, a2a_r, kv_s, kv_r, b_s, b_r, f_s, f_r, loc) = scratch
    row = lax.axis_index("row")
    x = lax.axis_index("col")
    c = row % 2
    z = row // 2 % NZ
    y = row // (2 * NZ)
    oc = 1 - c
    me = y * NZ + z
    near, far = c == 1, c == 0

    def dev(yy, zz, cc, xx):
        return ((yy * NZ + zz) * 2 + cc, xx)

    def wrap(v, n):
        return (v + n) % n

    def remote(src, dst, ssem, rsem, where):
        pltpu.make_async_remote_copy(
            src_ref=src, dst_ref=dst, send_sem=ssem, recv_sem=rsem, device_id=where, device_id_type=MESH
        ).start()

    def wait(ref, sem):
        pltpu.make_async_copy(ref, ref, sem).wait()

    flat = wb.reshape(NC * NX * FEAT * KT, LANE)

    def drain(sem, rows):
        wait(flat.at[pl.ds(0, rows)], sem)

    xp, xm, xo = wrap(x + 1, NX), wrap(x - 1, NX), wrap(x + 2, NX)
    yp, ym, yo = wrap(y + 1, NY), wrap(y - 1, NY), wrap(y + 2, NY)
    zp, zm = wrap(z + 1, NZ), wrap(z - 1, NZ)

    bar = pltpu.get_barrier_semaphore()

    def greet(k, carry):
        other = (me + k) % (NY * NZ)
        pl.semaphore_signal(bar, inc=1, device_id=(other * 2 + c, x), device_id_type=MESH)
        return carry

    lax.fori_loop(1, NY * NZ, greet, 0)
    for dx in range(NX):
        for dc in range(NC):
            if dx or dc:
                pl.semaphore_signal(
                    bar, inc=1, device_id=dev(y, z, (c + dc) % 2, (x + dx) % NX), device_id_type=MESH
                )
    pl.semaphore_wait(bar, NY * NZ - 1 + NX * NC - 1)

    for i in range(1, NX):
        xt = (x + i) % NX
        remote(act.at[xt], chunk.at[c, x], act_s.at[i], act_r.at[c, i], dev(y, z, 1, xt))

    @pl.when(far)
    def _():
        remote(act.at[x], chunk.at[0, x], act_s.at[0], act_r.at[0, 0], dev(y, z, 1, x))

    @pl.when(near)
    def _():
        pltpu.make_async_copy(act.at[x], chunk.at[1, x], act_r.at[1, 0]).start()

    def gather_start(src, buf, half, ss, rs, cs, cr, ls):
        for q, (first, target) in enumerate(((0, xp), (1, xm))):
            for p in (first, 1 - first):
                rows = pl.ds(p * half, half)
                remote(src.at[rows], buf.at[c, x, rows], ss, rs.at[q, p], dev(y, z, c, target))
        for p in range(2):
            rows = pl.ds(p * half, half)
            remote(src.at[rows], buf.at[c, x, rows], cs, cr.at[p], dev(y, z, oc, x))
        pltpu.make_async_copy(src, buf.at[c, x], ls).start()

    def gather_pass(buf, half, q, p, ss, rs, fr_, cs, cr):
        origin = xm if q == 0 else xp
        rows = pl.ds(p * half, half)
        piece = buf.at[c, origin, rows]
        wait(piece, rs.at[q, p])
        if p == q:
            remote(piece, piece, ss, fr_.at[q], dev(y, z, c, xp if q == 0 else xm))
        remote(piece, piece, cs, cr.at[2 + 2 * q + p], dev(y, z, oc, x))

    def gather_last(buf, half, fr_, cs, cr):
        for q in range(2):
            rows = pl.ds(q * half, half)
            piece = buf.at[c, xo, rows]
            wait(piece, fr_.at[q])
            remote(piece, piece, cs, cr.at[6 + q], dev(y, z, oc, x))

    def gather_core(buf, half, cr):
        for k, origin in enumerate((x, xm, xp, xo)):
            for p in range(2):
                wait(buf.at[oc, origin, pl.ds(p * half, half)], cr.at[2 * k + p])

    WH = FEAT * KT // 2
    OH = NOUT * 8 // 2
    W = (w_s, w_r, wf_r, wc_s, wc_r)
    O = (o_s, o_r, of_r, oc_s, oc_r)

    def wconv(d2, origin, p):
        def body(kt, carry):
            v = wb[d2, origin, pl.ds(p * WH + kt, FEAT // 2, stride=KT), :]
            hi, lo = split(v)
            lanes = pl.ds(pl.multiple_of(kt * LANE, LANE), LANE)
            at = pl.multiple_of(d2 * FEAT + p * (FEAT // 2), 16)
            whl[origin, pl.ds(at, FEAT // 2), lanes] = hi
            whl[origin, pl.ds(at + 2 * FEAT, FEAT // 2), lanes] = lo
            return carry

        lax.fori_loop(0, KT, body, 0)

    def weights(s):
        if s == 1:
            wait(w, loc.at[0])
            for p in range(2):
                wconv(c, x, p)
        if s == 2:
            gather_pass(wb, WH, 0, 0, *W)
            gather_pass(wb, WH, 1, 1, *W)
        if s == 3:
            wconv(c, xm, 0)
            wconv(c, xp, 1)
        if s == 4:
            for p in range(2):
                wait(wb.at[oc, x, pl.ds(p * WH, WH)], wc_r.at[p])
                wconv(oc, x, p)
        if s == 5:
            gather_pass(wb, WH, 0, 1, *W)
            gather_pass(wb, WH, 1, 0, *W)
            gather_start(ow, ob, OH, o_s, o_r, oc_s, oc_r, loc.at[1])
        if s == 6:
            wconv(c, xm, 1)
            wconv(c, xp, 0)
        if s == 7:
            for k, origin in ((1, xm), (2, xp)):
                for p in range(2):
                    wait(wb.at[oc, origin, pl.ds(p * WH, WH)], wc_r.at[2 * k + p])
                    wconv(oc, origin, p)
        if s == 8:
            gather_last(wb, WH, wf_r, wc_s, wc_r)
            for p in range(2):
                wconv(c, xo, p)
            for p in range(2):
                wait(wb.at[oc, xo, pl.ds(p * WH, WH)], wc_r.at[6 + p])
                wconv(oc, xo, p)
            gather_pass(ob, OH, 0, 0, *O)
            gather_pass(ob, OH, 1, 1, *O)

    gather_start(w, wb, WH, w_s, w_r, wc_s, wc_r, loc.at[0])

    def core(piece, sem):
        remote(piece, piece, c_s, sem, dev(y, z, 0, x))

    def back(d, s):
        return wrap(z - s, NZ) if d == 0 else wrap(z + s, NZ)

    def z1(cls, d, s, half=False):
        slot = back(d, s - 1)
        piece = g1.at[y, slot, cls, pl.ds(d * (R1 // 2), R1 // 2)] if half else g1.at[y, slot, cls]
        remote(piece, piece, z1_s, r1.at[cls, d, s - 1], dev(y, zp if d == 0 else zm, 1, x))

    def z2(cls, d, s, half=False):
        slot = back(d, s - 1)
        piece = g2.at[:, slot, cls, pl.ds(d * (R2 // 2), R2 // 2)] if half else g2.at[:, slot, cls]
        remote(piece, piece, z2_s, r2.at[cls, d, s - 1], dev(y, zp if d == 0 else zm, 1, x))

    def y1(slot):
        piece = g1.at[y, slot]
        remote(piece, piece, y_s, ry.at[0, slot], dev(yp, z, 1, x))
        remote(piece, piece, y_s, ry.at[1, slot], dev(ym, z, 1, x))
        core(g1.at[y, slot, 0], rc1.at[slot])

    def y1pass(slot):
        wait(g1.at[ym, slot], ry.at[0, slot])
        piece = g1.at[ym, slot, :, pl.ds(0, R1 // 2)]
        remote(piece, piece, h_s, rh.at[0, slot], dev(yp, z, 1, x))
        wait(g1.at[yp, slot], ry.at[1, slot])
        piece = g1.at[yp, slot, :, pl.ds(R1 // 2, R1 // 2)]
        remote(piece, piece, h_s, rh.at[1, slot], dev(ym, z, 1, x))
        core(g1.at[ym, slot, 0], rc1.at[slot])
        core(g1.at[yp, slot, 0], rc1.at[slot])

    def y1last(slot):
        wait(g1.at[yo, slot, :, pl.ds(0, R1 // 2)], rh.at[0, slot])
        wait(g1.at[yo, slot, :, pl.ds(R1 // 2, R1 // 2)], rh.at[1, slot])
        core(g1.at[yo, slot, 0], rc1.at[slot])

    @pl.when(near)
    def _():
        for cls in range(2):
            for i in range(NX):
                wait(chunk.at[0, 0], act_r.at[cls, i])
        for cls in range(2):
            data = chunk[cls]
            width = TILES * LANE

            def mean(v):
                return jnp.sum(jnp.sum(v, 0, keepdims=True), 2, keepdims=True) / width

            center = mean(data)
            scale = lax.rsqrt(mean(data * data) - center * center + EPS)
            normed = (data - center) * scale
            for t in range(TILES):
                v = normed[t // KT, :, t % KT * LANE : (t % KT + 1) * LANE]
                if 2 * t < R1:
                    g1[y, z, cls, pl.ds(2 * t, 2), :] = v
                else:
                    g2[y, z, cls, pl.ds(2 * t - R1, 2), :] = v
        for cls in range(2):
            for d in range(2):
                z1(cls, d, 1)
        own2 = g2.at[y, z]
        for k, target in enumerate((yp, ym, yo)):
            remote(own2, own2, p_s, rp.at[k], dev(target, z, 1, x))
        y1(z)
        for k, origin in enumerate((ym, yp, yo)):
            wait(g2.at[origin, z], rp.at[k])
        for cls in range(2):
            for d in range(2):
                z2(cls, d, 1)
        core(g2.at[:, z, 0], rc2.at[z])
        for s in range(1, 8):
            half = s == 7
            for cls in range(2):
                for d in range(2):
                    wait(g1.at[y, back(d, s), cls], r1.at[cls, d, s - 1])
                    z1(cls, d, s + 1, half)
            for d in range(2):
                y1(back(d, s))
            for cls in range(2):
                for d in range(2):
                    wait(g2.at[:, back(d, s), cls], r2.at[cls, d, s - 1])
                    z2(cls, d, s + 1, half)
            for d in range(2):
                core(g2.at[:, back(d, s), 0], rc2.at[back(d, s)])
            for d in range(1 if s == 1 else 2):
                y1pass(back(d, s - 1))
            if s > 1:
                for d in range(1 if s == 2 else 2):
                    y1last(back(d, s - 2))
            weights(s)
        opp = back(0, 8)
        for cls in range(2):
            for d in range(2):
                wait(g1.at[y, opp, cls, pl.ds(d * (R1 // 2), R1 // 2)], r1.at[cls, d, 7])
        y1(opp)
        for d in range(2):
            y1pass(back(d, 7))
        for cls in range(2):
            for d in range(2):
                wait(g2.at[:, opp, cls, pl.ds(d * (R2 // 2), R2 // 2)], r2.at[cls, d, 7])
        core(g2.at[:, opp, 0], rc2.at[opp])
        y1pass(opp)
        for d in range(2):
            y1last(back(d, 6))
        for d in range(2):
            y1last(back(d, 7))
        weights(8)
        y1last(opp)

    @pl.when(far)
    def _():
        for s in range(1, 9):
            weights(s)

        def arrive(slot, carry):
            wait(g1.at[:, slot, 0], rc1.at[slot])
            wait(g2.at[:, slot, 0], rc2.at[slot])
            return carry

        lax.fori_loop(0, NZ, arrive, 0)

    f1 = g1.reshape(NY * NZ * 2 * R1, LANE)
    f2 = g2.reshape(NY * NZ * 2 * R2, LANE)
    for t in range(TILES):
        for b in range(2):
            if 2 * t < R1:
                v = f1[pl.ds(c * R1 + 2 * t + b, NY * NZ, stride=2 * R1), :]
            else:
                v = f2[pl.ds(c * R2 + 2 * t - R1 + b, NY * NZ, stride=2 * R2), :]
            hi, lo = split(v)
            lanes = pl.ds(t % KT * LANE, LANE)
            ghl[t // KT, pl.ds(b * 64, 64), lanes] = hi
            ghl[t // KT, pl.ds(128 + b * 64, 64), lanes] = lo
    acc[...] = jnp.zeros_like(acc)

    def project(k, carry):
        acc[...] += lax.dot_general(
            whl[k], ghl[k], (((1,), (1,)), ((), ())), preferred_element_type=F32
        )
        return carry

    lax.fori_loop(0, NX, project, 0)
    full = acc[...]
    half_sum = full[:, :LANE] + full[:, LANE:]
    triples = half_sum[: 2 * FEAT] + half_sum[2 * FEAT :]

    msg[...] = jnp.zeros_like(msg)
    for d2 in range(2):
        for s in range(3):
            at = d2 * FEAT + s * HEADS
            msg[pl.ds(2 * s + d2, HEADS, stride=8), :] = triples[at : at + HEADS]

    def post(k, carry):
        h = (k + me // 2) % HEADS
        there = h // NZZ * NZ + h % NZZ * 2
        src = msg.at[pl.ds(pl.multiple_of(h * 8, 8), 8)]
        dst = rcv.at[pl.ds(pl.multiple_of(me * 8, 8), 8)]

        @pl.when(there != me)
        def _():
            remote(src, dst, a2a_s, a2a_r, (there * 2 + c, x))

        @pl.when(there == me)
        def _():
            pltpu.make_async_copy(src, dst, a2a_r).start()

        return carry

    lax.fori_loop(0, HEADS, post, 0)

    @pl.when(near)
    def _():
        drain(z1_s, 4 * (7 * R1 + R1 // 2))
        drain(z2_s, 4 * NY * (7 * R2 + R2 // 2))
        drain(y_s, NZ * 2 * 2 * R1)
        drain(h_s, NZ * 2 * R1)
        drain(c_s, NZ * NY * (R1 + R2))
        drain(p_s, 3 * 2 * R2)

    gather_pass(ob, OH, 0, 1, *O)
    gather_pass(ob, OH, 1, 0, *O)
    gather_last(ob, OH, of_r, oc_s, oc_r)
    wait(ow, loc.at[1])
    gather_core(ob, OH, oc_r)

    for d2 in range(2):
        for hq in range(NX):
            for j in range(8):
                v = ob[d2, hq, pl.ds(j, NOUT, stride=8), :]
                hi, lo = split(v)
                lanes = pl.ds(hq * LANE, LANE)
                owhl[j, pl.ds(d2 * NOUT, NOUT), lanes] = hi
                owhl[j, pl.ds(2 * NOUT + d2 * NOUT, NOUT), lanes] = lo

    even = z % 2 == 0
    odd = z % 2 == 1
    zz0 = z // 2

    def norm_rows(v):
        m = jnp.sum(v, 0, keepdims=True) / LANE
        q = jnp.sum(v * v, 0, keepdims=True) / LANE - m * m
        return (v - m) * lax.rsqrt(q + EPS)

    @pl.when(even)
    def _():
        wait(rcv, a2a_r)

        def part(s):
            return jnp.concatenate([rcv[pl.ds(2 * s + d2, 64, stride=8), :] for d2 in range(2)], 0)

        kv[c, pl.ds(0, LANE)] = norm_rows(part(1))
        kv[c, pl.ds(LANE, LANE)] = part(2)
        mine = kv.at[c]
        remote(mine, mine, kv_s, kv_r, dev(y, z, oc, x))
        queries = norm_rows(part(0)) * (LANE ** -0.5)
        wait(kv.at[oc], kv_r)
        es = []
        for k in range(2):
            keys = kv[k, pl.ds(0, LANE)].T
            es.append(jnp.exp(jnp.dot(keys, queries, precision=HIGHEST, preferred_element_type=F32)))
        norm = jnp.sum(es[0], 0, keepdims=True) + jnp.sum(es[1], 0, keepdims=True)
        o = sum(
            jnp.dot(kv[k, pl.ds(LANE, LANE)], es[k] / norm, precision=HIGHEST, preferred_element_type=F32)
            for k in range(2)
        )
        for d2 in range(2):
            att[zz0, y, c, pl.ds(d2, 64, stride=2), :] = o[d2 * 64 : d2 * 64 + 64]

    A2 = LANE - A1

    def slot_of(d, k):
        return wrap(zz0 - k, NZZ) if d == 0 else wrap((z + 1) // 2 + k, NZZ)

    def b1(cls, d, k, half=False):
        slot = slot_of(d, k)
        rows = pl.ds(d * (A1 // 2), A1 // 2) if half else pl.ds(0, A1)
        piece = att.at[slot, y, cls, rows]
        remote(piece, piece, z1_s, r1.at[cls, d, k], dev(y, zp if d == 0 else zm, 1, x))

    def b2(cls, d, k, half=False):
        slot = slot_of(d, k)
        rows = pl.ds(A1 + d * (A2 // 2), A2 // 2) if half else pl.ds(A1, A2)
        piece = att.at[slot, :, cls, rows]
        remote(piece, piece, z2_s, r2.at[cls, d, k], dev(y, zp if d == 0 else zm, 1, x))

    def v1(slot, own=False):
        piece = att.at[slot, y, :, pl.ds(0, A1)]
        remote(piece, piece, y_s, ry.at[0, slot], dev(yp, z, 1, x))
        remote(piece, piece, y_s, ry.at[1, slot], dev(ym, z, 1, x))
        if not own:
            core(att.at[slot, y, 0, pl.ds(0, A1)], rc1.at[slot])

    def v1pass(slot):
        wait(att.at[slot, ym, :, pl.ds(0, A1)], ry.at[0, slot])
        piece = att.at[slot, ym, :, pl.ds(0, A1 // 2)]
        remote(piece, piece, h_s, rh.at[0, slot], dev(yp, z, 1, x))
        wait(att.at[slot, yp, :, pl.ds(0, A1)], ry.at[1, slot])
        piece = att.at[slot, yp, :, pl.ds(A1 // 2, A1 // 2)]
        remote(piece, piece, h_s, rh.at[1, slot], dev(ym, z, 1, x))
        core(att.at[slot, ym, 0, pl.ds(0, A1)], rc1.at[slot])
        core(att.at[slot, yp, 0, pl.ds(0, A1)], rc1.at[slot])

    def v1last(slot):
        wait(att.at[slot, yo, :, pl.ds(0, A1 // 2)], rh.at[0, slot])
        wait(att.at[slot, yo, :, pl.ds(A1 // 2, A1 // 2)], rh.at[1, slot])
        core(att.at[slot, yo, 0, pl.ds(0, A1)], rc1.at[slot])

    acc2 = acc.at[pl.ds(0, 4 * NOUT)]
    acc2[...] = jnp.zeros((4 * NOUT, 2 * LANE), F32)

    def finish(slot, cls):
        block = att[slot, :, cls].reshape(NY * LANE, LANE)
        hi, lo = split(block)
        acc2[...] += jnp.dot(owhl[slot], jnp.concatenate([hi, lo], 1), preferred_element_type=F32)

    def z1wait(k, n):
        for cls in range(2):
            for d in range(2):
                wait(att.at[slot_of(d, k), y, cls, pl.ds(0, A1)], r1.at[cls, d, n])
                b1(cls, d, k, n == 3)
        for d in range(2):
            v1(slot_of(d, k))

    def z2wait(k, n):
        for cls in range(2):
            for d in range(2):
                wait(att.at[slot_of(d, k), :, cls, pl.ds(A1, A2)], r2.at[cls, d, n])
                b2(cls, d, k, n == 3)
        for d in range(2):
            core(att.at[slot_of(d, k), :, 0, pl.ds(A1, A2)], rc2.at[slot_of(d, k)])

    def lagged(slots):
        for slot in slots:
            v1pass(slot)
        for slot in slots:
            v1last(slot)
        for slot in slots:
            finish(slot, 1)

    @pl.when(near & even)
    def _():
        wait(att.at[zz0, y, 0], b_r)
        for cls in range(2):
            for d in range(2):
                b1(cls, d, 0)
        own = att.at[zz0, y, :, pl.ds(A1, A2)]
        for k, target in enumerate((yp, ym, yo)):
            remote(own, own, p_s, rp.at[k], dev(target, z, 1, x))
        v1(zz0, True)
        for k, origin in enumerate((ym, yp, yo)):
            wait(att.at[zz0, origin, :, pl.ds(A1, A2)], rp.at[k])
        for cls in range(2):
            for d in range(2):
                b2(cls, d, 0)
        for origin in (ym, yp, yo):
            core(att.at[zz0, origin, 0, pl.ds(A1, A2)], rc2.at[zz0])
        for k in range(1, 4):
            z1wait(k, k - 1)
            z2wait(k, k - 1)
            lagged([zz0] if k == 1 else [slot_of(0, k - 1), slot_of(1, k - 1)])
        slot = slot_of(0, 4)
        for cls in range(2):
            for d in range(2):
                wait(att.at[slot, y, cls, pl.ds(d * (A1 // 2), A1 // 2)], r1.at[cls, d, 3])
        v1(slot)
        for cls in range(2):
            for d in range(2):
                wait(att.at[slot, :, cls, pl.ds(A1 + d * (A2 // 2), A2 // 2)], r2.at[cls, d, 3])
        core(att.at[slot, :, 0, pl.ds(A1, A2)], rc2.at[slot])
        lagged([slot_of(0, 3), slot_of(1, 3)])
        lagged([slot])
        drain(p_s, 3 * 2 * A2)

    @pl.when(near & odd)
    def _():
        for k in range(4):
            z1wait(k, k)
            z2wait(k, k)
            if k:
                lagged([slot_of(0, k - 1), slot_of(1, k - 1)])
        lagged([slot_of(0, 3), slot_of(1, 3)])

    def from_near(slot):
        wait(att.at[slot, :, 0, pl.ds(0, A1)], rc1.at[slot])
        wait(att.at[slot, :, 0, pl.ds(A1, A2)], rc2.at[slot])
        finish(slot, 0)

    @pl.when(far & even)
    def _():
        own = att.at[zz0, y, 0]
        remote(own, own, b_s, b_r, dev(y, z, 1, x))
        wait(att.at[zz0, pl.ds(0, 3), 0, pl.ds(0, A1)], rc1.at[zz0])
        wait(att.at[zz0, pl.ds(0, 3), 0, pl.ds(A1, A2)], rc2.at[zz0])
        finish(zz0, 0)
        for k in range(1, 4):
            for d in range(2):
                from_near(slot_of(d, k))
        from_near(slot_of(0, 4))
        wait(own, b_s)

    @pl.when(far & odd)
    def _():
        for k in range(4):
            for d in range(2):
                from_near(slot_of(d, k))

    sums = acc2[...]
    sums = sums[:, :LANE] + sums[:, LANE:]
    sums = sums[: 2 * NOUT] + sums[2 * NOUT :]
    blocks = jnp.concatenate([sums, jnp.zeros((LANE - 2 * NOUT, LANE), F32)], 0).T
    for q in range(NX):
        for cc in range(NC):
            for b in range(2):
                at = b * 64 + q * 16
                fs[q, cc, pl.ds(b * 16, 16), pl.ds(0, NOUT)] = blocks[at : at + 16, cc * NOUT : cc * NOUT + NOUT]
    for dx in range(NX):
        for dc in range(NC):
            if dx or dc:
                tx, tc = (x + dx) % NX, (c + dc) % 2
                remote(fs.at[tx, tc], fr.at[x, c], f_s, f_r.at[dx, dc], dev(y, z, tc, tx))
    fr[x, c] = fs[x, c]
    for dx in range(NX):
        for dc in range(NC):
            if dx or dc:
                wait(fr.at[0, 0], f_r.at[dx, dc])
    for i in range(NX):
        for cc in range(NC):
            for b in range(2):
                out[i, pl.ds(2 * cc + b, 16, stride=4), :] = fr[i, cc, pl.ds(b * 16, 16), pl.ds(0, NOUT)]

    for i in range(1, NX):
        wait(chunk.at[0, 0], act_s.at[i])
    drain(w_s, 6 * WH)
    drain(wc_s, 8 * WH)
    drain(o_s, 6 * OH)
    drain(oc_s, 8 * OH)
    drain(f_s, 7 * 32)

    @pl.when(even)
    def _():
        drain(a2a_s, (HEADS - 1) * 8)
        wait(kv.at[0], kv_s)

    @pl.when(odd)
    def _():
        drain(a2a_s, HEADS * 8)

    @pl.when(far)
    def _():
        wait(chunk.at[0, 0], act_s.at[0])

    @pl.when(near)
    def _():
        drain(y_s, NZZ * 2 * 2 * A1)
        drain(h_s, NZZ * 2 * A1)

    @pl.when(near & even)
    def _():
        drain(z1_s, 16 * A1)
        drain(z2_s, 16 * NY * A2)
        drain(c_s, NZZ * NY * LANE - LANE)

    @pl.when(near & odd)
    def _():
        drain(z1_s, 14 * A1)
        drain(z2_s, 14 * NY * A2)
        drain(c_s, NZZ * NY * LANE)


def shards(activations, input_weight, output_weight):
    w = input_weight.reshape(FEAT * KT, LANE)
    ow = output_weight.reshape(NOUT * 8, LANE)
    dma = pltpu.SemaphoreType.DMA
    vm = pltpu.VMEM
    scratch = [
        vm((NC, NX, 2, KT * LANE), F32),
        vm((NY, NZ, NC, R1, LANE), F32),
        vm((NY, NZ, NC, R2, LANE), F32),
        vm((NC, NX, FEAT * KT, LANE), F32),
        vm((NX, 4 * FEAT, KT * LANE), BF16),
        vm((NX, 2 * LANE, KT * LANE), BF16),
        vm((NC, NX, NOUT * 8, LANE), F32),
        vm((NZZ, 4 * NOUT, NY * LANE), BF16),
        vm((HEADS * 8, LANE), F32),
        vm((NY * NZ * 8, LANE), F32),
        vm((NC, 2 * LANE, LANE), F32),
        vm((NZZ, NY, NC, LANE, LANE), F32),
        vm((NX, NC, 32, LANE), F32),
        vm((NX, NC, 32, LANE), F32),
        vm((4 * FEAT, 2 * LANE), F32),
        dma((NX,)), dma((NC, NX)),
        dma, dma((2, 2)), dma((2,)), dma, dma((8,)),
        dma, dma((2, 2)), dma((2,)), dma, dma((8,)),
        dma, dma, dma, dma, dma, dma,
        dma((2, 2, 8)), dma((2, 2, 8)),
        dma((2, NZ)), dma((2, NZ)), dma((3,)),
        dma((NZ,)), dma((NZ,)),
        dma, dma, dma, dma, dma, dma,
        dma, dma((NX, NC)),
        dma((2,)),
    ]
    return pl.pallas_call(
        kernel,
        out_shape=jax.ShapeDtypeStruct((NX, 64, NOUT), F32),
        in_specs=[
            pl.BlockSpec(memory_space=pl.ANY),
            pl.BlockSpec(memory_space=pl.ANY),
            pl.BlockSpec(memory_space=pl.ANY),
        ],
        out_specs=pl.BlockSpec(memory_space=pltpu.VMEM),
        scratch_shapes=scratch,
        compiler_params=pltpu.CompilerParams(
            collective_id=0, has_side_effects=True, vmem_limit_bytes=60 * 1024 * 1024
        ),
    )(activations, w, ow)


def solution(mesh):
    return jax.shard_map(
        shards,
        mesh=mesh,
        in_specs=(P(None, "row", "col"), P(None, None, "row", "col"), P("row", "col", None)),
        out_specs=P(None, "col", "row"),
        check_vma=False,
    )
```

```python
import jax
import jax.numpy as jnp
from jax import lax
from jax.experimental import pallas as pl
from jax.experimental.pallas import tpu as pltpu
from jax.sharding import PartitionSpec as P

MESH = pl.DeviceIdType.MESH
EPS = 1e-06
HIGHEST = lax.Precision.HIGHEST
F32 = jnp.float32
BF16 = jnp.bfloat16

NX, NY, NZ, NC = 4, 4, 16, 2
LANE = 128
TILES = 48
KT = TILES // NX
R = 2 * TILES
RA = 48
FAR = 5
HEADS = 32
NZZ = 8
A1 = 64
FEAT = 96
NOUT = 48


def split(x):
    hi = x.astype(BF16)
    return hi, (x - hi.astype(F32)).astype(BF16)


def kernel(act, w, ow, out, *scratch):
    (chunk, g, wb, whl, ghl, ob, owhl, msg, rcv, kv, att, fs, fr, acc,
     act_s, act_r, w_s, w_r, wf_r, wc_s, wc_r, o_s, o_r, of_r, oc_s, oc_r,
     z1_s, z2_s, y_s, h_s, c_s, p_s, r1, r2, ry, rh, rp, rc,
     a2a_s, a2a_r, kv_s, kv_r, b_s, b_r, f_s, f_r, loc) = scratch
    row = lax.axis_index("row")
    x = lax.axis_index("col")
    c = row % 2
    z = row // 2 % NZ
    y = row // (2 * NZ)
    oc = 1 - c
    me = y * NZ + z
    near, far = c == 1, c == 0

    def dev(yy, zz, cc, xx):
        return ((yy * NZ + zz) * 2 + cc, xx)

    def wrap(v, n):
        return (v + n) % n

    def remote(src, dst, ssem, rsem, where):
        pltpu.make_async_remote_copy(
            src_ref=src, dst_ref=dst, send_sem=ssem, recv_sem=rsem, device_id=where, device_id_type=MESH
        ).start()

    def wait(ref, sem):
        pltpu.make_async_copy(ref, ref, sem).wait()

    flat = wb.reshape(NC * NX * FEAT * KT, LANE)

    def drain(sem, rows):
        wait(flat.at[pl.ds(0, rows)], sem)

    xp, xm, xo = wrap(x + 1, NX), wrap(x - 1, NX), wrap(x + 2, NX)
    yp, ym, yo = wrap(y + 1, NY), wrap(y - 1, NY), wrap(y + 2, NY)
    zp, zm = wrap(z + 1, NZ), wrap(z - 1, NZ)

    bar = pltpu.get_barrier_semaphore()
    for dx in range(NX):
        for dc in range(NC):
            if dx or dc:
                pl.semaphore_signal(
                    bar, inc=1, device_id=dev(y, z, (c + dc) % 2, (x + dx) % NX), device_id_type=MESH
                )

    @pl.when(near)
    def _():
        for dz in (1, -1, FAR, -FAR):
            pl.semaphore_signal(bar, inc=1, device_id=dev(y, wrap(z + dz, NZ), 1, x), device_id_type=MESH)
        for yy in (yp, ym, yo):
            pl.semaphore_signal(bar, inc=1, device_id=dev(yy, z, 1, x), device_id_type=MESH)
        pl.semaphore_wait(bar, NX * NC - 1 + 4 + NY - 1)

    @pl.when(far)
    def _():
        pl.semaphore_wait(bar, NX * NC - 1)

    for i in range(1, NX):
        xt = (x + i) % NX
        remote(act.at[xt], chunk.at[c, x], act_s.at[i], act_r.at[c, i], dev(y, z, 1, xt))

    @pl.when(far)
    def _():
        remote(act.at[x], chunk.at[0, x], act_s.at[0], act_r.at[0, 0], dev(y, z, 1, x))

    @pl.when(near)
    def _():
        pltpu.make_async_copy(act.at[x], chunk.at[1, x], act_r.at[1, 0]).start()

    def gather_start(src, buf, half, ss, rs, cs, cr, ls):
        for q, (first, target) in enumerate(((0, xp), (1, xm))):
            for p in (first, 1 - first):
                rows = pl.ds(p * half, half)
                remote(src.at[rows], buf.at[c, x, rows], ss, rs.at[q, p], dev(y, z, c, target))
        for p in range(2):
            rows = pl.ds(p * half, half)
            remote(src.at[rows], buf.at[c, x, rows], cs, cr.at[p], dev(y, z, oc, x))
        pltpu.make_async_copy(src, buf.at[c, x], ls).start()

    def gather_pass(buf, half, q, p, ss, rs, fr_, cs, cr):
        origin = xm if q == 0 else xp
        rows = pl.ds(p * half, half)
        piece = buf.at[c, origin, rows]
        wait(piece, rs.at[q, p])
        if p == q:
            remote(piece, piece, ss, fr_.at[q], dev(y, z, c, xp if q == 0 else xm))
        remote(piece, piece, cs, cr.at[2 + 2 * q + p], dev(y, z, oc, x))

    def gather_last(buf, half, fr_, cs, cr):
        for q in range(2):
            rows = pl.ds(q * half, half)
            piece = buf.at[c, xo, rows]
            wait(piece, fr_.at[q])
            remote(piece, piece, cs, cr.at[6 + q], dev(y, z, oc, x))

    def gather_core(buf, half, cr):
        for k, origin in enumerate((x, xm, xp, xo)):
            for p in range(2):
                wait(buf.at[oc, origin, pl.ds(p * half, half)], cr.at[2 * k + p])

    WH = FEAT * KT // 2
    OH = NOUT * 8 // 2
    W = (w_s, w_r, wf_r, wc_s, wc_r)
    O = (o_s, o_r, of_r, oc_s, oc_r)

    def wconv(d2, origin, p):
        def body(kt, carry):
            v = wb[d2, origin, pl.ds(p * WH + kt, FEAT // 2, stride=KT), :]
            hi, lo = split(v)
            lanes = pl.ds(pl.multiple_of(kt * LANE, LANE), LANE)
            at = pl.multiple_of(d2 * FEAT + p * (FEAT // 2), 16)
            whl[origin, pl.ds(at, FEAT // 2), lanes] = hi
            whl[origin, pl.ds(at + 2 * FEAT, FEAT // 2), lanes] = lo
            return carry

        lax.fori_loop(0, KT, body, 0)

    def weights(s):
        if s == 1:
            wait(w, loc.at[0])
            for p in range(2):
                wconv(c, x, p)
        if s == 2:
            gather_pass(wb, WH, 0, 0, *W)
            gather_pass(wb, WH, 1, 1, *W)
        if s == 3:
            wconv(c, xm, 0)
            wconv(c, xp, 1)
        if s == 4:
            for p in range(2):
                wait(wb.at[oc, x, pl.ds(p * WH, WH)], wc_r.at[p])
                wconv(oc, x, p)
        if s == 5:
            gather_pass(wb, WH, 0, 1, *W)
            gather_pass(wb, WH, 1, 0, *W)
            gather_start(ow, ob, OH, o_s, o_r, oc_s, oc_r, loc.at[1])
        if s == 6:
            wconv(c, xm, 1)
            wconv(c, xp, 0)
        if s == 7:
            for k, origin in ((1, xm), (2, xp)):
                for p in range(2):
                    wait(wb.at[oc, origin, pl.ds(p * WH, WH)], wc_r.at[2 * k + p])
                    wconv(oc, origin, p)
        if s == 8:
            gather_last(wb, WH, wf_r, wc_s, wc_r)
            for p in range(2):
                wconv(c, xo, p)
            for p in range(2):
                wait(wb.at[oc, xo, pl.ds(p * WH, WH)], wc_r.at[6 + p])
                wconv(oc, xo, p)
            gather_pass(ob, OH, 0, 0, *O)
            gather_pass(ob, OH, 1, 1, *O)

    gather_start(w, wb, WH, w_s, w_r, wc_s, wc_r, loc.at[0])

    def core(piece, sem):
        remote(piece, piece, c_s, sem, dev(y, z, 0, x))

    def back(d, s):
        return wrap(z - s, NZ) if d == 0 else wrap(z + s, NZ)

    def onward(d, k):
        return dev(y, wrap(z + k, NZ) if d == 0 else wrap(z - k, NZ), 1, x)

    def z1(cls, d, s):
        if s < FAR:
            piece = g.at[y, back(d, s - 1), cls, pl.ds(0, RA)]
        elif s == FAR:
            piece = g.at[y, z, cls]
        elif s < NZ // 2:
            piece = g.at[y, back(d, s - 1), cls]
        else:
            piece = g.at[y, back(d, s - 1), cls, pl.ds(d * (R // 2), R // 2)]
        remote(piece, piece, z1_s, r1.at[cls, d, s - 1], onward(d, FAR if s == FAR else 1))

    def z1wait(cls, d, s):
        if s < FAR:
            piece = g.at[y, back(d, s), cls, pl.ds(0, RA)]
        elif s < NZ // 2:
            piece = g.at[y, back(d, s), cls]
        else:
            piece = g.at[y, back(d, s), cls, pl.ds(d * (R // 2), R // 2)]
        wait(piece, r1.at[cls, d, s - 1])

    def z2(cls, d, s):
        piece = g.at[:, back(d, s - 1), cls, pl.ds(RA, R - RA)]
        remote(piece, piece, z2_s, r2.at[cls, d, s - 1], onward(d, 1))

    def y1(slot, n):
        piece = g.at[y, slot, :, pl.ds(0, n)]
        remote(piece, piece, y_s, ry.at[0, slot], dev(yp, z, 1, x))
        remote(piece, piece, y_s, ry.at[1, slot], dev(ym, z, 1, x))
        core(g.at[y, slot, 0, pl.ds(0, n)], rc.at[slot])

    def y1pass(slot, n):
        wait(g.at[ym, slot, :, pl.ds(0, n)], ry.at[0, slot])
        piece = g.at[ym, slot, :, pl.ds(0, n // 2)]
        remote(piece, piece, h_s, rh.at[0, slot], dev(yp, z, 1, x))
        wait(g.at[yp, slot, :, pl.ds(0, n)], ry.at[1, slot])
        piece = g.at[yp, slot, :, pl.ds(n // 2, n // 2)]
        remote(piece, piece, h_s, rh.at[1, slot], dev(ym, z, 1, x))
        core(g.at[ym, slot, 0, pl.ds(0, n)], rc.at[slot])
        core(g.at[yp, slot, 0, pl.ds(0, n)], rc.at[slot])

    def y1last(slot, n):
        wait(g.at[yo, slot, :, pl.ds(0, n // 2)], rh.at[0, slot])
        wait(g.at[yo, slot, :, pl.ds(n // 2, n // 2)], rh.at[1, slot])
        core(g.at[yo, slot, 0, pl.ds(0, n)], rc.at[slot])

    def both(s):
        if s == 0:
            return [(z, RA)]
        if s == 4:
            return [(back(0, 8), R)] + [(back(d, 4), RA) for d in range(2)]
        return [(back(d, s + 4), R) for d in range(2)] + [(back(d, s), RA) for d in range(2)]

    @pl.when(near)
    def _():
        for cls in range(2):
            for i in range(NX):
                wait(chunk.at[0, 0], act_r.at[cls, i])
        for cls in range(2):
            data = chunk[cls]
            width = TILES * LANE

            def mean(v):
                return jnp.sum(jnp.sum(v, 0, keepdims=True), 2, keepdims=True) / width

            center = mean(data)
            scale = lax.rsqrt(mean(data * data) - center * center + EPS)
            normed = (data - center) * scale
            for t in range(TILES):
                v = normed[t // KT, :, t % KT * LANE : (t % KT + 1) * LANE]
                g[y, z, cls, pl.ds(2 * t, 2), :] = v
        for s in (FAR, 1):
            for cls in range(2):
                for d in range(2):
                    z1(cls, d, s)
        own2 = g.at[y, z, :, pl.ds(RA, R - RA)]
        for k, target in enumerate((yp, ym, yo)):
            remote(own2, own2, p_s, rp.at[k], dev(target, z, 1, x))
        y1(z, RA)
        for k, origin in enumerate((ym, yp, yo)):
            wait(g.at[origin, z, :, pl.ds(RA, R - RA)], rp.at[k])
        for cls in range(2):
            for d in range(2):
                z2(cls, d, 1)
        core(g.at[:, z, 0, pl.ds(RA, R - RA)], rc.at[z])
        weights(1)
        for s in range(1, 5):
            for q in (s + 4, s):
                for cls in range(2):
                    for d in range(2):
                        z1wait(cls, d, q)
                        if s < 4:
                            z1(cls, d, q + 1)
            for slot, n in both(s):
                y1(slot, n)
            for slot, n in both(s - 1):
                y1pass(slot, n)
            for cls in range(2):
                for d in range(2):
                    wait(g.at[:, back(d, s), cls, pl.ds(RA, R - RA)], r2.at[cls, d, s - 1])
                    if s < 4:
                        z2(cls, d, s + 1)
            for d in range(2):
                core(g.at[:, back(d, s), 0, pl.ds(RA, R - RA)], rc.at[back(d, s)])
            if s > 1:
                for slot, n in both(s - 2):
                    y1last(slot, n)
            for k in ((2, 3), (4,), (5, 6), (7,))[s - 1]:
                weights(k)
        for slot, n in both(4):
            y1pass(slot, n)
        for slot, n in both(3) + both(4):
            y1last(slot, n)
        weights(8)

    @pl.when(far)
    def _():
        for s in range(1, 9):
            weights(s)

        def arrive(slot, carry):
            wait(g.at[:, slot, 0], rc.at[slot])
            return carry

        lax.fori_loop(0, NZ, arrive, 0)

    flat_g = g.reshape(NY * NZ * NC * R, LANE)
    for t in range(TILES):
        for b in range(2):
            v = flat_g[pl.ds(c * R + 2 * t + b, NY * NZ, stride=NC * R), :]
            hi, lo = split(v)
            lanes = pl.ds(t % KT * LANE, LANE)
            ghl[t // KT, pl.ds(b * 64, 64), lanes] = hi
            ghl[t // KT, pl.ds(128 + b * 64, 64), lanes] = lo
    acc[...] = jnp.zeros_like(acc)

    def project(k, carry):
        acc[...] += lax.dot_general(
            whl[k], ghl[k], (((1,), (1,)), ((), ())), preferred_element_type=F32
        )
        return carry

    lax.fori_loop(0, NX, project, 0)
    full = acc[...]
    half_sum = full[:, :LANE] + full[:, LANE:]
    triples = half_sum[: 2 * FEAT] + half_sum[2 * FEAT :]

    msg[...] = jnp.zeros_like(msg)
    for d2 in range(2):
        for s in range(3):
            at = d2 * FEAT + s * HEADS
            msg[pl.ds(2 * s + d2, HEADS, stride=8), :] = triples[at : at + HEADS]

    def post(k, carry):
        h = (k + me // 2) % HEADS
        there = h // NZZ * NZ + h % NZZ * 2
        src = msg.at[pl.ds(pl.multiple_of(h * 8, 8), 8)]
        dst = rcv.at[pl.ds(pl.multiple_of(me * 8, 8), 8)]

        @pl.when(there != me)
        def _():
            remote(src, dst, a2a_s, a2a_r, (there * 2 + c, x))

        @pl.when(there == me)
        def _():
            pltpu.make_async_copy(src, dst, a2a_r).start()

        return carry

    lax.fori_loop(0, HEADS, post, 0)

    @pl.when(near)
    def _():
        drain(z1_s, 4 * (4 * RA + 3 * R + R // 2))
        drain(z2_s, 4 * 4 * NY * (R - RA))
        drain(y_s, 4 * (9 * RA + 7 * R))
        drain(h_s, 2 * (9 * RA + 7 * R))
        drain(c_s, NZ * NY * R)
        drain(p_s, 3 * 2 * (R - RA))

    gather_pass(ob, OH, 0, 1, *O)
    gather_pass(ob, OH, 1, 0, *O)
    gather_last(ob, OH, of_r, oc_s, oc_r)
    wait(ow, loc.at[1])
    gather_core(ob, OH, oc_r)

    for d2 in range(2):
        for hq in range(NX):
            for j in range(8):
                v = ob[d2, hq, pl.ds(j, NOUT, stride=8), :]
                hi, lo = split(v)
                lanes = pl.ds(hq * LANE, LANE)
                owhl[j, pl.ds(d2 * NOUT, NOUT), lanes] = hi
                owhl[j, pl.ds(2 * NOUT + d2 * NOUT, NOUT), lanes] = lo

    even = z % 2 == 0
    odd = z % 2 == 1
    zz0 = z // 2

    def norm_rows(v):
        m = jnp.sum(v, 0, keepdims=True) / LANE
        q = jnp.sum(v * v, 0, keepdims=True) / LANE - m * m
        return (v - m) * lax.rsqrt(q + EPS)

    @pl.when(even)
    def _():
        wait(rcv, a2a_r)

        def part(s):
            return jnp.concatenate([rcv[pl.ds(2 * s + d2, 64, stride=8), :] for d2 in range(2)], 0)

        kv[c, pl.ds(0, LANE)] = norm_rows(part(1))
        kv[c, pl.ds(LANE, LANE)] = part(2)
        mine = kv.at[c]
        remote(mine, mine, kv_s, kv_r, dev(y, z, oc, x))
        queries = norm_rows(part(0)) * (LANE ** -0.5)
        wait(kv.at[oc], kv_r)
        es = []
        for k in range(2):
            keys = kv[k, pl.ds(0, LANE)].T
            es.append(jnp.exp(jnp.dot(keys, queries, precision=HIGHEST, preferred_element_type=F32)))
        norm = jnp.sum(es[0], 0, keepdims=True) + jnp.sum(es[1], 0, keepdims=True)
        o = sum(
            jnp.dot(kv[k, pl.ds(LANE, LANE)], es[k] / norm, precision=HIGHEST, preferred_element_type=F32)
            for k in range(2)
        )
        for d2 in range(2):
            att[zz0, y, c, pl.ds(d2, 64, stride=2), :] = o[d2 * 64 : d2 * 64 + 64]

    def slot_of(d, s):
        return back(d, s) // 2

    def b1(cls, d, s):
        if s < FAR:
            piece = att.at[slot_of(d, s - 1), y, cls, pl.ds(0, A1)]
        elif s < NZ // 2:
            piece = att.at[slot_of(d, s - 1 if s > FAR else 0), y, cls]
        else:
            piece = att.at[slot_of(d, s - 1), y, cls, pl.ds(d * (LANE // 2), LANE // 2)]
        remote(piece, piece, z1_s, r1.at[cls, d, s - 1], onward(d, FAR if s == FAR else 1))

    def b1wait(cls, d, s):
        if s < FAR:
            piece = att.at[slot_of(d, s), y, cls, pl.ds(0, A1)]
        elif s < NZ // 2:
            piece = att.at[slot_of(d, s), y, cls]
        else:
            piece = att.at[slot_of(d, s), y, cls, pl.ds(d * (LANE // 2), LANE // 2)]
        wait(piece, r1.at[cls, d, s - 1])

    def b2(cls, d, s):
        piece = att.at[slot_of(d, s - 1), :, cls, pl.ds(A1, LANE - A1)]
        remote(piece, piece, z2_s, r2.at[cls, d, s - 1], onward(d, 1))

    def v1(slot, n, own=False):
        piece = att.at[slot, y, :, pl.ds(0, n)]
        remote(piece, piece, y_s, ry.at[0, slot], dev(yp, z, 1, x))
        remote(piece, piece, y_s, ry.at[1, slot], dev(ym, z, 1, x))
        if not own:
            core(att.at[slot, y, 0, pl.ds(0, n)], rc.at[slot])

    def v1pass(slot, n):
        wait(att.at[slot, ym, :, pl.ds(0, n)], ry.at[0, slot])
        piece = att.at[slot, ym, :, pl.ds(0, n // 2)]
        remote(piece, piece, h_s, rh.at[0, slot], dev(yp, z, 1, x))
        wait(att.at[slot, yp, :, pl.ds(0, n)], ry.at[1, slot])
        piece = att.at[slot, yp, :, pl.ds(n // 2, n // 2)]
        remote(piece, piece, h_s, rh.at[1, slot], dev(ym, z, 1, x))
        core(att.at[slot, ym, 0, pl.ds(0, n)], rc.at[slot])
        core(att.at[slot, yp, 0, pl.ds(0, n)], rc.at[slot])

    def v1last(slot, n):
        wait(att.at[slot, yo, :, pl.ds(0, n // 2)], rh.at[0, slot])
        wait(att.at[slot, yo, :, pl.ds(n // 2, n // 2)], rh.at[1, slot])
        core(att.at[slot, yo, 0, pl.ds(0, n)], rc.at[slot])

    def places(s):
        if s == 0:
            return [(zz0, A1)]
        if s == 4:
            return [(slot_of(0, 8), LANE)] + [(slot_of(d, 4), A1) for d in range(2)]
        return [(slot_of(d, s + 4), LANE) for d in range(2)] + [(slot_of(d, s), A1) for d in range(2)]

    acc2 = acc.at[pl.ds(0, 4 * NOUT)]
    acc2[...] = jnp.zeros((4 * NOUT, 2 * LANE), F32)

    def finish(slot, cls):
        block = att[slot, :, cls].reshape(NY * LANE, LANE)
        hi, lo = split(block)
        acc2[...] += jnp.dot(owhl[slot], jnp.concatenate([hi, lo], 1), preferred_element_type=F32)

    def round_of(s, before):
        for q in (s + 4, s):
            for cls in range(2):
                for d in range(2):
                    b1wait(cls, d, q)
                    if s < 4:
                        b1(cls, d, q + 1)
        for slot, n in places(s):
            v1(slot, n)
        for slot, n in before:
            v1pass(slot, n)
        for cls in range(2):
            for d in range(2):
                wait(att.at[slot_of(d, s), :, cls, pl.ds(A1, LANE - A1)], r2.at[cls, d, s - 1])
                if s < 4:
                    b2(cls, d, s + 1)
        for d in range(2):
            core(att.at[slot_of(d, s), :, 0, pl.ds(A1, LANE - A1)], rc.at[slot_of(d, s)])
        for slot, n in before:
            v1last(slot, n)
        for slot, n in before:
            finish(slot, 1)

    def last_of(slots):
        for slot, n in slots:
            v1pass(slot, n)
        for slot, n in slots:
            v1last(slot, n)
        for slot, n in slots:
            finish(slot, 1)

    @pl.when(near & even)
    def _():
        wait(att.at[zz0, y, 0], b_r)
        for s in (FAR, 1):
            for cls in range(2):
                for d in range(2):
                    b1(cls, d, s)
        own = att.at[zz0, y, :, pl.ds(A1, LANE - A1)]
        for k, target in enumerate((yp, ym, yo)):
            remote(own, own, p_s, rp.at[k], dev(target, z, 1, x))
        v1(zz0, A1, True)
        for k, origin in enumerate((ym, yp, yo)):
            wait(att.at[zz0, origin, :, pl.ds(A1, LANE - A1)], rp.at[k])
        for cls in range(2):
            for d in range(2):
                b2(cls, d, 1)
        for origin in (ym, yp, yo):
            core(att.at[zz0, origin, 0, pl.ds(A1, LANE - A1)], rc.at[zz0])
        round_of(2, places(0))
        round_of(4, places(2))
        last_of(places(4))

    @pl.when(near & odd)
    def _():
        round_of(1, [])
        round_of(3, places(1))
        last_of(places(3))

    def from_near(slot):
        wait(att.at[slot, :, 0], rc.at[slot])
        finish(slot, 0)

    @pl.when(far & even)
    def _():
        own = att.at[zz0, y, 0]
        remote(own, own, b_s, b_r, dev(y, z, 1, x))
        wait(att.at[zz0, pl.ds(0, 3), 0], rc.at[zz0])
        finish(zz0, 0)
        for s in (2, 4):
            for slot, n in places(s):
                from_near(slot)
        wait(own, b_s)

    @pl.when(far & odd)
    def _():
        for s in (1, 3):
            for slot, n in places(s):
                from_near(slot)

    sums = acc2[...]
    sums = sums[:, :LANE] + sums[:, LANE:]
    sums = sums[: 2 * NOUT] + sums[2 * NOUT :]
    blocks = jnp.concatenate([sums, jnp.zeros((LANE - 2 * NOUT, LANE), F32)], 0).T
    for q in range(NX):
        for cc in range(NC):
            for b in range(2):
                at = b * 64 + q * 16
                fs[q, cc, pl.ds(b * 16, 16), pl.ds(0, NOUT)] = blocks[at : at + 16, cc * NOUT : cc * NOUT + NOUT]
    for dx in range(NX):
        for dc in range(NC):
            if dx or dc:
                tx, tc = (x + dx) % NX, (c + dc) % 2
                remote(fs.at[tx, tc], fr.at[x, c], f_s, f_r.at[dx, dc], dev(y, z, tc, tx))
    fr[x, c] = fs[x, c]
    for dx in range(NX):
        for dc in range(NC):
            if dx or dc:
                wait(fr.at[0, 0], f_r.at[dx, dc])
    for i in range(NX):
        for cc in range(NC):
            for b in range(2):
                out[i, pl.ds(2 * cc + b, 16, stride=4), :] = fr[i, cc, pl.ds(b * 16, 16), pl.ds(0, NOUT)]

    for i in range(1, NX):
        wait(chunk.at[0, 0], act_s.at[i])
    drain(w_s, 6 * WH)
    drain(wc_s, 8 * WH)
    drain(o_s, 6 * OH)
    drain(oc_s, 8 * OH)
    drain(f_s, 7 * 32)

    @pl.when(even)
    def _():
        drain(a2a_s, (HEADS - 1) * 8)
        wait(kv.at[0], kv_s)

    @pl.when(odd)
    def _():
        drain(a2a_s, HEADS * 8)

    @pl.when(far)
    def _():
        wait(chunk.at[0, 0], act_s.at[0])

    @pl.when(near & even)
    def _():
        drain(z1_s, 8 * A1 + 8 * LANE)
        drain(z2_s, 8 * NY * (LANE - A1))
        drain(y_s, 4 * (5 * A1 + 3 * LANE))
        drain(h_s, 2 * (5 * A1 + 3 * LANE))
        drain(c_s, NZZ * NY * LANE - LANE)
        drain(p_s, 3 * 2 * (LANE - A1))

    @pl.when(near & odd)
    def _():
        drain(z1_s, 8 * A1 + 6 * LANE)
        drain(z2_s, 8 * NY * (LANE - A1))
        drain(y_s, 4 * (4 * A1 + 4 * LANE))
        drain(h_s, 2 * (4 * A1 + 4 * LANE))
        drain(c_s, NZZ * NY * LANE)


def shards(activations, input_weight, output_weight):
    w = input_weight.reshape(FEAT * KT, LANE)
    ow = output_weight.reshape(NOUT * 8, LANE)
    dma = pltpu.SemaphoreType.DMA
    vm = pltpu.VMEM
    scratch = [
        vm((NC, NX, 2, KT * LANE), F32),
        vm((NY, NZ, NC, R, LANE), F32),
        vm((NC, NX, FEAT * KT, LANE), F32),
        vm((NX, 4 * FEAT, KT * LANE), BF16),
        vm((NX, 2 * LANE, KT * LANE), BF16),
        vm((NC, NX, NOUT * 8, LANE), F32),
        vm((NZZ, 4 * NOUT, NY * LANE), BF16),
        vm((HEADS * 8, LANE), F32),
        vm((NY * NZ * 8, LANE), F32),
        vm((NC, 2 * LANE, LANE), F32),
        vm((NZZ, NY, NC, LANE, LANE), F32),
        vm((NX, NC, 32, LANE), F32),
        vm((NX, NC, 32, LANE), F32),
        vm((4 * FEAT, 2 * LANE), F32),
        dma((NX,)), dma((NC, NX)),
        dma, dma((2, 2)), dma((2,)), dma, dma((8,)),
        dma, dma((2, 2)), dma((2,)), dma, dma((8,)),
        dma, dma, dma, dma, dma, dma,
        dma((2, 2, 8)), dma((2, 2, 4)),
        dma((2, NZ)), dma((2, NZ)), dma((3,)),
        dma((NZ,)),
        dma, dma, dma, dma, dma, dma,
        dma, dma((NX, NC)),
        dma((2,)),
    ]
    return pl.pallas_call(
        kernel,
        out_shape=jax.ShapeDtypeStruct((NX, 64, NOUT), F32),
        in_specs=[
            pl.BlockSpec(memory_space=pl.ANY),
            pl.BlockSpec(memory_space=pl.ANY),
            pl.BlockSpec(memory_space=pl.ANY),
        ],
        out_specs=pl.BlockSpec(memory_space=pltpu.VMEM),
        scratch_shapes=scratch,
        compiler_params=pltpu.CompilerParams(
            collective_id=0, has_side_effects=True, vmem_limit_bytes=60 * 1024 * 1024
        ),
    )(activations, w, ow)


def solution(mesh):
    return jax.shard_map(
        shards,
        mesh=mesh,
        in_specs=(P(None, "row", "col"), P(None, None, "row", "col"), P("row", "col", None)),
        out_specs=P(None, "col", "row"),
        check_vma=False,
    )
```

```python
import jax
import jax.numpy as jnp
from jax import lax
from jax.experimental import pallas as pl
from jax.experimental.pallas import tpu as pltpu
from jax.sharding import PartitionSpec as P

MESH = pl.DeviceIdType.MESH
EPS = 1e-06
HIGHEST = lax.Precision.HIGHEST
F32 = jnp.float32
BF16 = jnp.bfloat16

NX, NY, NZ, NC = 4, 4, 16, 2
LANE = 128
TILES = 48
KT = TILES // NX
R = 2 * TILES
R1, R2 = 64, 32
STRAIGHT = 7
STREAMS = 4
HEADS = 32
NZZ = 8
A1 = 80
FEAT = 96
NOUT = 48


def split(x):
    hi = x.astype(BF16)
    return hi, (x - hi.astype(F32)).astype(BF16)


def kernel(act, w, ow, out, *scratch):
    (chunk, g, wb, whl, ghl, ob, owhl, msg, rcv, kv, att, fs, fr, turn, acc,
     act_s, act_r, w_s, w_r, wf_r, wn_s, wn_r, o_s, o_r, of_r, on_s, on_r,
     z1_s, z2_s, y_s, h_s, c_s, c2_s, p_s, r1, r2, ry, rh, rp, rc,
     a2a_s, a2a_r, kv_s, kv_r, b_s, b_r, f_s, f_r, loc) = scratch
    row = lax.axis_index("row")
    x = lax.axis_index("col")
    c = row % 2
    z = row // 2 % NZ
    y = row // (2 * NZ)
    me = y * NZ + z
    near, far = c == 1, c == 0
    even, odd = z % 2 == 0, z % 2 == 1
    zz0 = z // 2

    def dev(yy, zz, cc, xx):
        return ((yy * NZ + zz) * 2 + cc, xx)

    def wrap(v, n):
        return (v + n) % n

    def remote(src, dst, ssem, rsem, where):
        pltpu.make_async_remote_copy(
            src_ref=src, dst_ref=dst, send_sem=ssem, recv_sem=rsem, device_id=where, device_id_type=MESH
        ).start()

    def wait(ref, sem):
        pltpu.make_async_copy(ref, ref, sem).wait()

    flat = wb.reshape(NC * NX * FEAT * KT, LANE)

    def drain(sem, rows):
        wait(flat.at[pl.ds(0, rows)], sem)

    xp, xm, xo = wrap(x + 1, NX), wrap(x - 1, NX), wrap(x + 2, NX)
    yp, ym, yo = wrap(y + 1, NY), wrap(y - 1, NY), wrap(y + 2, NY)

    bar = pltpu.get_barrier_semaphore()

    def greet(where):
        pl.semaphore_signal(bar, inc=1, device_id=where, device_id_type=MESH)

    @pl.when(near)
    def _():
        greet(dev(y, z, 0, x))
        for i in range(1, NX):
            for cc in range(NC):
                greet(dev(y, z, cc, wrap(x + i, NX)))
        for dz in (1, -1):
            greet(dev(y, wrap(z + dz, NZ), 1, x))
        for yy in (yp, ym, yo):
            greet(dev(yy, z, 1, x))
        pl.semaphore_wait(bar, 1 + NX - 1 + 2 + NY - 1)

    @pl.when(far)
    def _():
        greet(dev(y, z, 1, x))
        for xx in (xp, xm):
            greet(dev(y, z, 0, xx))
        pl.semaphore_wait(bar, NX + 2)

    for i in range(1, NX):
        xt = (x + i) % NX
        remote(act.at[xt], chunk.at[c, x], act_s.at[i], act_r.at[c, i], dev(y, z, 1, xt))

    @pl.when(far)
    def _():
        remote(act.at[x], chunk.at[0, x], act_s.at[0], act_r.at[0, 0], dev(y, z, 1, x))

    @pl.when(near)
    def _():
        pltpu.make_async_copy(act.at[x], chunk.at[1, x], act_r.at[1, 0]).start()
        remote(w, wb.at[1, x], wn_s, wn_r, dev(y, z, 0, x))
        remote(ow, ob.at[1, x], on_s, on_r, dev(y, z, 0, x))

    def gather_send(src, buf, d2, half, ss, rs):
        for q, (first, target) in enumerate(((0, xp), (1, xm))):
            for p in (first, 1 - first):
                rows = pl.ds(p * half, half)
                remote(src.at[rows], buf.at[d2, x, rows], ss, rs.at[d2, q, p], dev(y, z, 0, target))

    def gather_pass(buf, d2, half, q, p, ss, rs, fr_):
        origin = xm if q == 0 else xp
        piece = buf.at[d2, origin, pl.ds(p * half, half)]
        wait(piece, rs.at[d2, q, p])
        if p == q:
            remote(piece, piece, ss, fr_.at[d2, q], dev(y, z, 0, xp if q == 0 else xm))

    def gather_last(buf, d2, half, q, fr_):
        wait(buf.at[d2, xo, pl.ds(q * half, half)], fr_.at[d2, q])

    WH = FEAT * KT // 2
    OH = NOUT * 8 // 2

    def wconv(d2, origin, p):
        def body(kt, carry):
            v = wb[d2, origin, pl.ds(p * WH + kt, FEAT // 2, stride=KT), :]
            hi, lo = split(v)
            lanes = pl.ds(pl.multiple_of(kt * LANE, LANE), LANE)
            at = d2 * FEAT + p * (FEAT // 2)
            whl[origin, pl.ds(at, FEAT // 2), lanes] = hi
            whl[origin, pl.ds(at + 2 * FEAT, FEAT // 2), lanes] = lo
            return carry

        lax.fori_loop(0, KT, body, 0)

    def core(piece, sem, sent):
        remote(piece, piece, sent, sem, dev(y, z, 0, x))

    def back(d, s):
        return wrap(z - s, NZ) if d == 0 else wrap(z + s, NZ)

    def onward(d, k):
        return dev(y, wrap(z + k, NZ) if d == 0 else wrap(z - k, NZ), 1, x)

    ONES = pl.ds(0, R1)
    TWOS = pl.ds(R1, R2)

    def cutting(d, s, first, n):
        if s < NZ // 2:
            return pl.ds(first, n)
        share = (n // 2 + 7) // 8 * 8
        return pl.ds(first + share, n - share) if d else pl.ds(first, share)

    def z1piece(u, d, s, t):
        n = R1 // 2
        return g.at[back(d, s - t), y, u // 2, cutting(d, s, u % 2 * n, n)]

    def z2piece(u, d, s, t):
        return g.at[back(d, s - t), pl.ds(u % 2 * 2, 2), u // 2, cutting(d, s, R1, R2)]

    def z1(u, d, s):
        piece = z1piece(u, d, s, 1)
        remote(piece, piece, z1_s, r1.at[u, d, s - 1], onward(d, 1))

    def z2(u, d, s):
        piece = z2piece(u, d, s, 1)
        remote(piece, piece, z2_s, r2.at[u, d, s - 1], onward(d, 1))

    def y1(slot, straight):
        piece = g.at[slot, y, :, ONES]
        remote(piece, piece, y_s, ry.at[0, slot], dev(yp, z, 1, x))
        remote(piece, piece, y_s, ry.at[1, slot], dev(ym, z, 1, x))
        if straight:
            remote(piece, piece, y_s, rh.at[0, slot], dev(yo, z, 1, x))
        core(piece, rc.at[slot], c_s)

    def y1pass(slot, straight):
        for q, origin, target in ((0, ym, yp), (1, yp, ym)):
            wait(g.at[slot, origin, :, ONES], ry.at[q, slot])
            if not straight:
                piece = g.at[slot, origin, :, pl.ds(q * (R1 // 2), R1 // 2)]
                remote(piece, piece, h_s, rh.at[q, slot], dev(target, z, 1, x))
        core(g.at[slot, ym, :, ONES], rc.at[slot], c_s)
        core(g.at[slot, yp, :, ONES], rc.at[slot], c_s)

    def y1last(slot, straight):
        if straight:
            wait(g.at[slot, yo, :, ONES], rh.at[0, slot])
        else:
            for q in range(2):
                wait(g.at[slot, yo, :, pl.ds(q * (R1 // 2), R1 // 2)], rh.at[q, slot])
        core(g.at[slot, yo, :, ONES], rc.at[slot], c_s)

    def spots(s):
        if s in (0, NZ // 2):
            return [(back(0, s), s >= STRAIGHT)]
        return [(back(d, s), s >= STRAIGHT) for d in range(2)]

    @pl.when(near)
    def _():
        for cls in range(2):
            for i in range(NX):
                wait(chunk.at[0, 0], act_r.at[cls, i])
        for cls in range(2):
            data = chunk[cls]
            width = TILES * LANE

            def mean(v):
                return jnp.sum(jnp.sum(v, 0, keepdims=True), 2, keepdims=True) / width

            center = mean(data)
            scale = lax.rsqrt(mean(data * data) - center * center + EPS)
            normed = (data - center) * scale
            for t in range(TILES):
                v = normed[t // KT, :, t % KT * LANE : (t % KT + 1) * LANE]
                g[z, y, cls, pl.ds(2 * t, 2), :] = v
            for u in (2 * cls, 2 * cls + 1):
                for d in range(2):
                    z1(u, d, 1)
        own2 = g.at[z, y, :, TWOS]
        for k, target in enumerate((yp, ym, yo)):
            remote(own2, own2, p_s, rp.at[k], dev(target, z, 1, x))
        y1(z, False)
        for k, origin in enumerate((ym, yp, yo)):
            wait(g.at[z, origin, :, TWOS], rp.at[k])
        for u in range(STREAMS):
            for d in range(2):
                z2(u, d, 1)
        core(g.at[z, :, :, TWOS], rc.at[z], c2_s)
        last = NZ // 2
        for s in range(1, last + 4):
            if s <= last:
                for u in range(STREAMS):
                    for d in range(2):
                        wait(z1piece(u, d, s, 0), r1.at[u, d, s - 1])
                        if s < last:
                            z1(u, d, s + 1)
                for spot in spots(s):
                    y1(*spot)
            t = s - 1
            if 1 <= t <= last:
                for u in range(STREAMS):
                    for d in range(2):
                        wait(z2piece(u, d, t, 0), r2.at[u, d, t - 1])
                        if t < last:
                            z2(u, d, t + 1)
                for slot, _ in spots(t):
                    core(g.at[slot, :, :, TWOS], rc.at[slot], c2_s)
            if 0 <= s - 2 <= last:
                for spot in spots(s - 2):
                    y1pass(*spot)
            if 0 <= s - 3 <= last:
                for spot in spots(s - 3):
                    y1last(*spot)

    @pl.when(far)
    def _():
        own = pltpu.make_async_copy(w, wb.at[0, x], loc.at[0])
        own.start()
        gather_send(w, wb, 0, WH, w_s, w_r)
        wait(wb.at[1, x], wn_r)
        gather_send(wb.at[1, x], wb, 1, WH, w_s, w_r)
        own.wait()
        for d2 in range(2):
            for p in range(2):
                wconv(d2, x, p)
        for p in range(2):
            for d2 in range(2):
                gather_pass(wb, d2, WH, 0, p, w_s, w_r, wf_r)
                gather_pass(wb, d2, WH, 1, 1 - p, w_s, w_r, wf_r)
            for d2 in range(2):
                wconv(d2, xm, p)
                wconv(d2, xp, 1 - p)
        own = pltpu.make_async_copy(ow, ob.at[0, x], loc.at[1])
        own.start()
        gather_send(ow, ob, 0, OH, o_s, o_r)
        wait(ob.at[1, x], on_r)
        gather_send(ob.at[1, x], ob, 1, OH, o_s, o_r)
        for d2 in range(2):
            for q in range(2):
                gather_last(wb, d2, WH, q, wf_r)
                wconv(d2, xo, q)
        own.wait()

        flat_g = g.reshape(NZ * NY * NC * R, LANE)

        def arrive(k, carry):
            away = (k + 1) // 2
            slot = wrap(z + away - 2 * away * (k % 2), NZ)
            wait(g.at[slot], rc.at[slot])
            rows = pl.ds(pl.multiple_of(slot * 16, 16), 16)
            low = pl.ds(pl.multiple_of(2 * LANE + slot * 16, 16), 16)
            for t in range(TILES):
                v = jnp.concatenate(
                    [flat_g[pl.ds(slot * (NY * NC * R) + 2 * t + b, NY * NC, stride=R), :] for b in range(2)], 0
                )
                hi, lo = split(v)
                lanes = pl.ds(t % KT * LANE, LANE)
                ghl[t // KT, rows, lanes] = hi
                ghl[t // KT, low, lanes] = lo
            return carry

        lax.fori_loop(0, NZ, arrive, 0)

        acc[...] = jnp.zeros_like(acc)
        turned = (((1,), (1,)), ((), ()))

        def project(k, carry):
            acc[...] += lax.dot_general(whl[k, : 2 * FEAT], ghl[k], turned, preferred_element_type=F32)
            acc[:, :256] += lax.dot_general(
                whl[k, 2 * FEAT :], ghl[k, :256], turned, preferred_element_type=F32
            )
            return carry

        lax.fori_loop(0, NX, project, 0)
        triples = acc[:, :256] + acc[:, 256:]

        msg[...] = jnp.zeros_like(msg)
        for cls in range(2):
            for d2 in range(2):
                for s in range(3):
                    at = d2 * FEAT + s * HEADS
                    msg[cls, pl.ds(2 * s + d2, HEADS, stride=8), :] = triples[
                        at : at + HEADS, cls * LANE : (cls + 1) * LANE
                    ]

        def post(k, carry):
            h = (k + me // 2) % HEADS
            there = h // NZZ * NZ + h % NZZ * 2
            rows = pl.ds(pl.multiple_of(h * 8, 8), 8)
            dst = rcv.at[pl.ds(pl.multiple_of(me * 8, 8), 8)]
            remote(msg.at[1, rows], dst, a2a_s, a2a_r, (there * 2 + 1, x))

            @pl.when(there != me)
            def _():
                remote(msg.at[0, rows], dst, a2a_s, a2a_r, (there * 2, x))

            @pl.when(there == me)
            def _():
                pltpu.make_async_copy(msg.at[0, rows], dst, a2a_r).start()

            return carry

        lax.fori_loop(0, HEADS, post, 0)

        for p in range(2):
            for d2 in range(2):
                gather_pass(ob, d2, OH, 0, p, o_s, o_r, of_r)
                gather_pass(ob, d2, OH, 1, 1 - p, o_s, o_r, of_r)
        for d2 in range(2):
            for q in range(2):
                gather_last(ob, d2, OH, q, of_r)

        for d2 in range(2):
            for hq in range(NX):
                for j in range(8):
                    hi, lo = split(ob[d2, hq, pl.ds(j, NOUT, stride=8), :])
                    lanes = pl.ds(hq * LANE, LANE)
                    owhl[j, pl.ds(d2 * NOUT, NOUT), lanes] = hi
                    owhl[j, pl.ds(2 * NOUT + d2 * NOUT, NOUT), lanes] = lo

    @pl.when(near)
    def _():
        drain(z1_s, 4 * (7 * R1 + R1 // 2))
        drain(z2_s, 4 * NY * (7 * R2 + R2 // 2))
        straight = 2 * (NZ // 2 - STRAIGHT) + 1
        drain(y_s, (NZ * 2 + straight) * 2 * R1)
        drain(h_s, (NZ - straight) * 2 * R1)
        drain(c_s, NZ * NY * NC * R1)
        drain(c2_s, NZ * NY * NC * R2)
        drain(p_s, 3 * 2 * R2)

    def norm_rows(v):
        m = jnp.sum(v, 0, keepdims=True) / LANE
        q = jnp.sum(v * v, 0, keepdims=True) / LANE - m * m
        return (v - m) * lax.rsqrt(q + EPS)

    @pl.when(even)
    def _():
        wait(rcv, a2a_r)

        def third(s):
            return jnp.concatenate([rcv[pl.ds(2 * s + d2, 64, stride=8), :] for d2 in range(2)], 0)

        kv[c, pl.ds(0, LANE)] = norm_rows(third(1))
        kv[c, pl.ds(LANE, LANE)] = third(2)
        mine = kv.at[c]
        remote(mine, mine, kv_s, kv_r, dev(y, z, 1 - c, x))
        queries = norm_rows(third(0)) * (LANE ** -0.5)
        wait(kv.at[1 - c], kv_r)
        es = []
        for k in range(2):
            keys = kv[k, pl.ds(0, LANE)].T
            es.append(jnp.exp(jnp.dot(keys, queries, precision=HIGHEST, preferred_element_type=F32)))
        norm = jnp.sum(es[0], 0, keepdims=True) + jnp.sum(es[1], 0, keepdims=True)
        o = sum(
            jnp.dot(kv[k, pl.ds(LANE, LANE)], es[k] / norm, precision=HIGHEST, preferred_element_type=F32)
            for k in range(2)
        )
        for d2 in range(2):
            att[zz0, y, c, pl.ds(d2, 64, stride=2), :] = o[d2 * 64 : d2 * 64 + 64]

    def slot_of(d, s):
        return back(d, s) // 2

    def b1piece(u, d, s, t):
        n = A1 // 2
        return att.at[slot_of(d, s - t), y, u // 2, cutting(d, s, u % 2 * n, n)]

    def b2piece(u, d, s, t):
        return att.at[slot_of(d, s - t), pl.ds(u % 2 * 2, 2), u // 2, cutting(d, s, A1, LANE - A1)]

    def b1(u, d, s):
        piece = b1piece(u, d, s, 1)
        remote(piece, piece, z1_s, r1.at[u, d, s - 1], onward(d, 1))

    def b2(u, d, s):
        piece = b2piece(u, d, s, 1)
        remote(piece, piece, z2_s, r2.at[u, d, s - 1], onward(d, 1))

    FIRST = pl.ds(0, A1)
    SECOND = pl.ds(A1, LANE - A1)

    def v1(slot, straight, own=False):
        piece = att.at[slot, y, :, FIRST]
        remote(piece, piece, y_s, ry.at[0, slot], dev(yp, z, 1, x))
        remote(piece, piece, y_s, ry.at[1, slot], dev(ym, z, 1, x))
        if straight:
            remote(piece, piece, y_s, rh.at[0, slot], dev(yo, z, 1, x))
        if not own:
            core(piece, rc.at[slot], c_s)

    def v1pass(slot, straight):
        for q, origin, target in ((0, ym, yp), (1, yp, ym)):
            wait(att.at[slot, origin, :, FIRST], ry.at[q, slot])
            if not straight:
                piece = att.at[slot, origin, :, pl.ds(q * (A1 // 2), A1 // 2)]
                remote(piece, piece, h_s, rh.at[q, slot], dev(target, z, 1, x))
        core(att.at[slot, ym, :, FIRST], rc.at[slot], c_s)
        core(att.at[slot, yp, :, FIRST], rc.at[slot], c_s)

    def v1last(slot, straight):
        if straight:
            wait(att.at[slot, yo, :, FIRST], rh.at[0, slot])
        else:
            for q in range(2):
                wait(att.at[slot, yo, :, pl.ds(q * (A1 // 2), A1 // 2)], rh.at[q, slot])
        core(att.at[slot, yo, :, FIRST], rc.at[slot], c_s)

    def places(s):
        if s in (0, NZ // 2):
            return [(slot_of(0, s), s >= STRAIGHT)]
        return [(slot_of(d, s), s >= STRAIGHT) for d in range(2)]

    ACROSS = pl.ds(0, 2 * NOUT)

    @pl.when(far)
    def _():
        acc[ACROSS] = jnp.zeros((2 * NOUT, 4 * LANE), F32)

    def finish(slot):
        halves = [split(att[slot, :, cls].reshape(NY * LANE, LANE)) for cls in range(2)]
        hi = jnp.concatenate([h for h, _ in halves], 1)
        lo = jnp.concatenate([l for _, l in halves], 1)
        acc[ACROSS] += jnp.dot(
            owhl[slot, : 2 * NOUT], jnp.concatenate([hi, lo], 1), preferred_element_type=F32
        )
        acc[ACROSS, : 2 * LANE] += jnp.dot(owhl[slot, 2 * NOUT :], hi, preferred_element_type=F32)

    def round_of(s, before, earlier):
        last = NZ // 2
        for u in range(STREAMS):
            for d in range(2):
                wait(b1piece(u, d, s, 0), r1.at[u, d, s - 1])
                if s < last:
                    b1(u, d, s + 1)
        for place in places(s):
            v1(*place)
        for place in before:
            v1pass(*place)
        for u in range(STREAMS):
            for d in range(2):
                wait(b2piece(u, d, s, 0), r2.at[u, d, s - 1])
                if s < last:
                    b2(u, d, s + 1)
        for slot, _ in places(s):
            core(att.at[slot, :, :, SECOND], rc.at[slot], c_s)
        for place in earlier:
            v1last(*place)

    def last_of(before, earlier):
        for place in before:
            v1pass(*place)
        for place in earlier:
            v1last(*place)

    @pl.when(near & even)
    def _():
        core(att.at[zz0, y, 1], rc.at[zz0], c_s)
        wait(att.at[zz0, y, 0], b_r)
        for u in range(STREAMS):
            for d in range(2):
                b1(u, d, 1)
        own = att.at[zz0, y, :, SECOND]
        for k, target in enumerate((yp, ym, yo)):
            remote(own, own, p_s, rp.at[k], dev(target, z, 1, x))
        v1(zz0, False, True)
        for k, origin in enumerate((ym, yp, yo)):
            wait(att.at[zz0, origin, :, SECOND], rp.at[k])
        for u in range(STREAMS):
            for d in range(2):
                b2(u, d, 1)
        for origin in (ym, yp, yo):
            core(att.at[zz0, origin, :, SECOND], rc.at[zz0], c_s)
        round_of(2, places(0), [])
        round_of(4, places(2), places(0))
        round_of(6, places(4), places(2))
        round_of(8, places(6), places(4))
        last_of(places(8), places(6) + places(8))

    @pl.when(near & odd)
    def _():
        round_of(1, [], [])
        round_of(3, places(1), [])
        round_of(5, places(3), places(1))
        round_of(7, places(5), places(3))
        last_of(places(7), places(5) + places(7))

    def from_near(slot):
        wait(att.at[slot], rc.at[slot])
        finish(slot)

    @pl.when(far & even)
    def _():
        own = att.at[zz0, y, 0]
        remote(own, own, b_s, b_r, dev(y, z, 1, x))
        drain(rc.at[zz0], (2 * NY - 1) * LANE)
        finish(zz0)
        for s in (2, 4, 6, 8):
            for slot, _ in places(s):
                from_near(slot)
        wait(own, b_s)

    @pl.when(far & odd)
    def _():
        for s in (1, 3, 5, 7):
            for slot, _ in places(s):
                from_near(slot)

    @pl.when(far)
    def _():
        sums = acc[ACROSS, : 2 * LANE] + acc[ACROSS, 2 * LANE :]
        for k in range(2):
            mine = sums[:, k * LANE : (k + 1) * LANE]
            turn[pl.ds(k * LANE, LANE)] = jnp.concatenate([mine, jnp.zeros((LANE - 2 * NOUT, LANE), F32)], 0).T
        for q in range(NX):
            for cls in range(NC):
                mine = turn[pl.ds(q * NC + cls, 2 * NZ, stride=NY * NC), :]
                for cc in range(NC):
                    fs[q, cc, pl.ds(cls * 32, 32), pl.ds(0, NOUT)] = mine[:, cc * NOUT : cc * NOUT + NOUT]
        for dx in (2, 1, 3, 0):
            for cc in range(NC):
                if dx or cc:
                    tx = (x + dx) % NX
                    remote(fs.at[tx, cc], fr.at[x], f_s, f_r.at[dx], dev(y, z, cc, tx))
        fr[x] = fs[x, 0]

    @pl.when(near)
    def _():
        wait(fr.at[0], f_r.at[0])

    for dx in range(1, NX):
        wait(fr.at[0], f_r.at[dx])
    for i in range(NX):
        for cls in range(NC):
            for b in range(2):
                out[i, pl.ds(2 * cls + b, 16, stride=4), :] = fr[i, pl.ds(cls * 32 + b, 16, stride=2), :][:, :NOUT]

    for i in range(1, NX):
        wait(chunk.at[0, 0], act_s.at[i])

    @pl.when(even)
    def _():
        wait(kv.at[0], kv_s)

    @pl.when(far)
    def _():
        wait(chunk.at[0, 0], act_s.at[0])
        drain(w_s, 12 * WH)
        drain(o_s, 12 * OH)
        drain(f_s, 7 * 64)

    @pl.when(far & even)
    def _():
        drain(a2a_s, (2 * HEADS - 1) * 8)

    @pl.when(far & odd)
    def _():
        drain(a2a_s, 2 * HEADS * 8)

    @pl.when(near)
    def _():
        drain(wn_s, 2 * WH)
        drain(on_s, 2 * OH)

    @pl.when(near & even)
    def _():
        drain(z1_s, 2 * NC * 4 * A1)
        drain(z2_s, 2 * NC * 4 * NY * (LANE - A1))
        drain(y_s, (NZZ * 2 + 1) * 2 * A1)
        drain(h_s, (NZZ - 1) * 2 * A1)
        drain(c_s, NZZ * NY * NC * LANE - LANE)
        drain(p_s, 3 * 2 * (LANE - A1))

    @pl.when(near & odd)
    def _():
        up, down = 24, 16
        drain(z1_s, NC * (2 * 3 * A1 + 2 * up + 2 * down))
        drain(z2_s, NC * 7 * NY * (LANE - A1))
        drain(y_s, (NZZ * 2 + 2) * 2 * A1)
        drain(h_s, (NZZ - 2) * 2 * A1)
        drain(c_s, NZZ * NY * NC * LANE)


def shards(activations, input_weight, output_weight):
    w = input_weight.reshape(FEAT * KT, LANE)
    ow = output_weight.reshape(NOUT * 8, LANE)
    dma = pltpu.SemaphoreType.DMA
    vm = pltpu.VMEM
    scratch = [
        vm((NC, NX, 2, KT * LANE), F32),
        vm((NZ, NY, NC, R, LANE), F32),
        vm((NC, NX, FEAT * KT, LANE), F32),
        vm((NX, 4 * FEAT, KT * LANE), BF16),
        vm((NX, 4 * LANE, KT * LANE), BF16),
        vm((NC, NX, NOUT * 8, LANE), F32),
        vm((NZZ, 4 * NOUT, NY * LANE), BF16),
        vm((NC, HEADS * 8, LANE), F32),
        vm((NY * NZ * 8, LANE), F32),
        vm((NC, 2 * LANE, LANE), F32),
        vm((NZZ, NY, NC, LANE, LANE), F32),
        vm((NX, NC, 64, LANE), F32),
        vm((NX, 64, LANE), F32),
        vm((2 * LANE, LANE), F32),
        vm((2 * FEAT, 4 * LANE), F32),
        dma((NX,)), dma((NC, NX)),
        dma, dma((2, 2, 2)), dma((2, 2)), dma, dma,
        dma, dma((2, 2, 2)), dma((2, 2)), dma, dma,
        dma, dma, dma, dma, dma, dma, dma,
        dma((STREAMS, 2, 8)), dma((STREAMS, 2, 8)),
        dma((2, NZ)), dma((2, NZ)), dma((3,)),
        dma((NZ,)),
        dma, dma, dma, dma, dma, dma,
        dma, dma((NX,)),
        dma((2,)),
    ]
    return pl.pallas_call(
        kernel,
        out_shape=jax.ShapeDtypeStruct((NX, 64, NOUT), F32),
        in_specs=[
            pl.BlockSpec(memory_space=pl.ANY),
            pl.BlockSpec(memory_space=pl.ANY),
            pl.BlockSpec(memory_space=pl.ANY),
        ],
        out_specs=pl.BlockSpec(memory_space=pltpu.VMEM),
        scratch_shapes=scratch,
        compiler_params=pltpu.CompilerParams(
            collective_id=0, has_side_effects=True, vmem_limit_bytes=60 * 1024 * 1024
        ),
    )(activations, w, ow)


def solution(mesh):
    return jax.shard_map(
        shards,
        mesh=mesh,
        in_specs=(P(None, "row", "col"), P(None, None, "row", "col"), P("row", "col", None)),
        out_specs=P(None, "col", "row"),
        check_vma=False,
    )
```

```python
import jax
import jax.numpy as jnp
from jax import lax
from jax.experimental import pallas as pl
from jax.experimental.pallas import tpu as pltpu
from jax.sharding import PartitionSpec as P

MESH = pl.DeviceIdType.MESH
EPS = 1e-06
HIGHEST = lax.Precision.HIGHEST
F32 = jnp.float32
BF16 = jnp.bfloat16

NX, NY, NZ, NC = 4, 4, 16, 2
LANE = 128
TILES = 48
KT = TILES // NX
R = 2 * TILES
R1, R2 = 72, 24
STRAIGHT = 7
STREAMS = 2
PER = STREAMS // 2
HEADS = 32
NZZ = 8
A1 = 104
FEAT = 96
NOUT = 48


def split(x):
    hi = x.astype(BF16)
    return hi, (x - hi.astype(F32)).astype(BF16)


def kernel(act, w, ow, out, *scratch):
    (chunk, g, wb, whl, ghl, ob, owhl, msg, rcv, kv, att, fs, fr, turn, acc,
     act_s, act_r, w_s, w_r, wf_r, wn_s, wn_r, o_s, o_r, of_r, on_s, on_r,
     z1_s, z2_s, y_s, h_s, c_s, c2_s, p_s, r1, r2, ry, rh, rp, rc,
     a2a_s, a2a_r, kv_s, kv_r, b_s, b_r, f_s, f_r, loc) = scratch
    row = lax.axis_index("row")
    x = lax.axis_index("col")
    c = row % 2
    z = row // 2 % NZ
    y = row // (2 * NZ)
    me = y * NZ + z
    near, far = c == 1, c == 0
    even, odd = z % 2 == 0, z % 2 == 1

    def dev(yy, zz, cc, xx):
        return ((yy * NZ + zz) * 2 + cc, xx)

    def wrap(v, n):
        return (v + n) % n

    def remote(src, dst, ssem, rsem, where):
        pltpu.make_async_remote_copy(
            src_ref=src, dst_ref=dst, send_sem=ssem, recv_sem=rsem, device_id=where, device_id_type=MESH
        ).start()

    def wait(ref, sem):
        pltpu.make_async_copy(ref, ref, sem).wait()

    flat = wb.reshape(NC * NX * FEAT * KT, LANE)

    def drain(sem, rows):
        wait(flat.at[pl.ds(0, rows)], sem)

    xp, xm, xo = wrap(x + 1, NX), wrap(x - 1, NX), wrap(x + 2, NX)
    yp, ym, yo = wrap(y + 1, NY), wrap(y - 1, NY), wrap(y + 2, NY)

    bar = pltpu.get_barrier_semaphore()

    def greet(where):
        pl.semaphore_signal(bar, inc=1, device_id=where, device_id_type=MESH)

    @pl.when(near)
    def _():
        greet(dev(y, z, 0, x))
        for i in range(1, NX):
            for cc in range(NC):
                greet(dev(y, z, cc, wrap(x + i, NX)))
        for dz in (1, -1):
            greet(dev(y, wrap(z + dz, NZ), 1, x))
        for yy in (yp, ym, yo):
            greet(dev(yy, z, 1, x))
        pl.semaphore_wait(bar, 1 + NX - 1 + 2 + NY - 1)

    @pl.when(far)
    def _():
        greet(dev(y, z, 1, x))
        for xx in (xp, xm):
            greet(dev(y, z, 0, xx))
        pl.semaphore_wait(bar, NX + 2)

    for i in range(1, NX):
        xt = (x + i) % NX
        remote(act.at[xt], chunk.at[c, x], act_s.at[i], act_r.at[c, i], dev(y, z, 1, xt))

    @pl.when(far)
    def _():
        remote(act.at[x], chunk.at[0, x], act_s.at[0], act_r.at[0, 0], dev(y, z, 1, x))

    @pl.when(near)
    def _():
        pltpu.make_async_copy(act.at[x], chunk.at[1, x], act_r.at[1, 0]).start()
        remote(w, wb.at[1, x], wn_s, wn_r, dev(y, z, 0, x))
        remote(ow, ob.at[1, x], on_s, on_r, dev(y, z, 0, x))

    def gather_send(src, buf, d2, half, ss, rs):
        for q, (first, target) in enumerate(((0, xp), (1, xm))):
            for p in (first, 1 - first):
                rows = pl.ds(p * half, half)
                remote(src.at[rows], buf.at[d2, x, rows], ss, rs.at[d2, q, p], dev(y, z, 0, target))

    def gather_pass(buf, d2, half, q, p, ss, rs, fr_):
        origin = xm if q == 0 else xp
        piece = buf.at[d2, origin, pl.ds(p * half, half)]
        wait(piece, rs.at[d2, q, p])
        if p == q:
            remote(piece, piece, ss, fr_.at[d2, q], dev(y, z, 0, xp if q == 0 else xm))

    def gather_last(buf, d2, half, q, fr_):
        wait(buf.at[d2, xo, pl.ds(q * half, half)], fr_.at[d2, q])

    WH = FEAT * KT // 2
    OH = NOUT * 8 // 2

    def wconv(d2, origin, p):
        def body(kt, carry):
            v = wb[d2, origin, pl.ds(p * WH + kt, FEAT // 2, stride=KT), :]
            hi, lo = split(v)
            lanes = pl.ds(pl.multiple_of(kt * LANE, LANE), LANE)
            at = d2 * FEAT + p * (FEAT // 2)
            whl[origin, pl.ds(at, FEAT // 2), lanes] = hi
            whl[origin, pl.ds(at + 2 * FEAT, FEAT // 2), lanes] = lo
            return carry

        lax.fori_loop(0, KT, body, 0)

    def ysplit(q, n):
        share = (n // 2 + 7) // 8 * 8
        return pl.ds(share, n - share) if q else pl.ds(0, share)

    def core(piece, sem, sent):
        remote(piece, piece, sent, sem, to_far)

    def place(d, s):
        return (NZ - s) % NZ if d else s

    def back(d, s):
        return wrap(z - s, NZ) if d == 0 else wrap(z + s, NZ)

    toward = [dev(y, wrap(z + 1, NZ), 1, x), dev(y, wrap(z - 1, NZ), 1, x)]
    to_yp, to_ym, to_yo = [dev(yy, z, 1, x) for yy in (yp, ym, yo)]
    to_far = dev(y, z, 0, x)

    ONES = pl.ds(0, R1)
    TWOS = pl.ds(R1, R2)

    def cutting(d, s, first, n):
        if s < NZ // 2:
            return pl.ds(first, n)
        share = (n // 2 + 7) // 8 * 8
        return pl.ds(first + share, n - share) if d else pl.ds(first, share)

    def z1piece(u, d, s, t):
        n = R1 // PER
        return g.at[place(d, s - t), y, u // PER, cutting(d, s, u % PER * n, n)]

    def z2piece(u, d, s, t):
        return g.at[place(d, s - t), pl.ds(u % PER * (NY // PER), NY // PER), u // PER, cutting(d, s, R1, R2)]

    def z1(u, d, s):
        remote(z1piece(u, d, s, 1), z1piece(u, d, s, 0), z1_s, r1.at[u, d, s - 1], toward[d])

    def z2(u, d, s):
        remote(z2piece(u, d, s, 1), z2piece(u, d, s, 0), z2_s, r2.at[u, d, s - 1], toward[d])

    def y1(slot, straight):
        piece = g.at[slot, y, :, ONES]
        remote(piece, piece, y_s, ry.at[0, slot], to_yp)
        remote(piece, piece, y_s, ry.at[1, slot], to_ym)
        if straight:
            remote(piece, piece, y_s, rh.at[0, slot], to_yo)
        core(piece, rc.at[slot], c_s)

    def y1pass(slot, straight):
        for q, origin, target in ((0, ym, to_yp), (1, yp, to_ym)):
            wait(g.at[slot, origin, :, ONES], ry.at[q, slot])
            if not straight:
                piece = g.at[slot, origin, :, ysplit(q, R1)]
                remote(piece, piece, h_s, rh.at[q, slot], target)
        core(g.at[slot, ym, :, ONES], rc.at[slot], c_s)
        core(g.at[slot, yp, :, ONES], rc.at[slot], c_s)

    def y1last(slot, straight):
        if straight:
            wait(g.at[slot, yo, :, ONES], rh.at[0, slot])
        else:
            for q in range(2):
                wait(g.at[slot, yo, :, ysplit(q, R1)], rh.at[q, slot])
        core(g.at[slot, yo, :, ONES], rc.at[slot], c_s)

    def spots(s):
        return [(p, s >= STRAIGHT) for p in sorted({place(d, s) for d in range(2)})]

    @pl.when(near)
    def _():
        for cls in range(2):
            for i in range(NX):
                wait(chunk.at[0, 0], act_r.at[cls, i])
        for cls in range(2):
            data = chunk[cls]
            width = TILES * LANE

            def mean(v):
                return jnp.sum(jnp.sum(v, 0, keepdims=True), 2, keepdims=True) / width

            center = mean(data)
            scale = lax.rsqrt(mean(data * data) - center * center + EPS)
            normed = (data - center) * scale
            for t in range(TILES):
                v = normed[t // KT, :, t % KT * LANE : (t % KT + 1) * LANE]
                g[0, y, cls, pl.ds(2 * t, 2), :] = v
            for u in range(PER * cls, PER * cls + PER):
                for d in range(2):
                    z1(u, d, 1)
        own2 = g.at[0, y, :, TWOS]
        for k, target in enumerate((to_yp, to_ym, to_yo)):
            remote(own2, own2, p_s, rp.at[k], target)
        y1(0, False)
        for k, origin in enumerate((ym, yp, yo)):
            wait(g.at[0, origin, :, TWOS], rp.at[k])
        for u in range(STREAMS):
            for d in range(2):
                z2(u, d, 1)
        core(g.at[0, :, :, TWOS], rc.at[0], c2_s)
        last = NZ // 2
        for s in range(1, last + 4):
            if s <= last:
                for u in range(STREAMS):
                    for d in range(2):
                        wait(z1piece(u, d, s, 0), r1.at[u, d, s - 1])
                        if s < last:
                            z1(u, d, s + 1)
                for spot in spots(s):
                    y1(*spot)
            t = s - 1
            if 1 <= t <= last:
                for u in range(STREAMS):
                    for d in range(2):
                        wait(z2piece(u, d, t, 0), r2.at[u, d, t - 1])
                        if t < last:
                            z2(u, d, t + 1)
                for slot, _ in spots(t):
                    core(g.at[slot, :, :, TWOS], rc.at[slot], c2_s)
            if 0 <= s - 2 <= last:
                for spot in spots(s - 2):
                    y1pass(*spot)
            if 0 <= s - 3 <= last:
                for spot in spots(s - 3):
                    y1last(*spot)

    @pl.when(far)
    def _():
        own = pltpu.make_async_copy(w, wb.at[0, x], loc.at[0])
        own.start()
        gather_send(w, wb, 0, WH, w_s, w_r)
        wait(wb.at[1, x], wn_r)
        gather_send(wb.at[1, x], wb, 1, WH, w_s, w_r)
        own.wait()
        for d2 in range(2):
            for p in range(2):
                wconv(d2, x, p)
        for p in range(2):
            for d2 in range(2):
                gather_pass(wb, d2, WH, 0, p, w_s, w_r, wf_r)
                gather_pass(wb, d2, WH, 1, 1 - p, w_s, w_r, wf_r)
            for d2 in range(2):
                wconv(d2, xm, p)
                wconv(d2, xp, 1 - p)
        own = pltpu.make_async_copy(ow, ob.at[0, x], loc.at[1])
        own.start()
        gather_send(ow, ob, 0, OH, o_s, o_r)
        wait(ob.at[1, x], on_r)
        gather_send(ob.at[1, x], ob, 1, OH, o_s, o_r)
        for d2 in range(2):
            for q in range(2):
                gather_last(wb, d2, WH, q, wf_r)
                wconv(d2, xo, q)
        own.wait()

        flat_g = g.reshape(NZ * NY * NC * R, LANE)

        def arrive(k, carry):
            away = (k + 1) // 2
            lies = away + (NZ - 2 * away) * (k % 2)
            slot = wrap(z - away + 2 * away * (k % 2), NZ)
            wait(g.at[lies], rc.at[lies])
            rows = pl.ds(pl.multiple_of(slot * 16, 16), 16)
            low = pl.ds(pl.multiple_of(2 * LANE + slot * 16, 16), 16)
            for t in range(TILES):
                v = jnp.concatenate(
                    [flat_g[pl.ds(lies * (NY * NC * R) + 2 * t + b, NY * NC, stride=R), :] for b in range(2)], 0
                )
                hi, lo = split(v)
                lanes = pl.ds(t % KT * LANE, LANE)
                ghl[t // KT, rows, lanes] = hi
                ghl[t // KT, low, lanes] = lo
            return carry

        lax.fori_loop(0, NZ, arrive, 0)

        acc[...] = jnp.zeros_like(acc)
        turned = (((1,), (1,)), ((), ()))

        def project(k, carry):
            acc[...] += lax.dot_general(whl[k, : 2 * FEAT], ghl[k], turned, preferred_element_type=F32)
            acc[:, :256] += lax.dot_general(
                whl[k, 2 * FEAT :], ghl[k, :256], turned, preferred_element_type=F32
            )
            return carry

        lax.fori_loop(0, NX, project, 0)
        triples = acc[:, :256] + acc[:, 256:]

        msg[...] = jnp.zeros_like(msg)
        for cls in range(2):
            for d2 in range(2):
                for s in range(3):
                    at = d2 * FEAT + s * HEADS
                    msg[cls, pl.ds(2 * s + d2, HEADS, stride=8), :] = triples[
                        at : at + HEADS, cls * LANE : (cls + 1) * LANE
                    ]

        def post(k, carry):
            j = k // NY
            zz = (z // 2 + 4 + (j + 1) // 2 * (1 - 2 * (j % 2))) % NZZ
            yy = (y + 2 + k) % NY
            h = yy * NZZ + zz
            there = yy * NZ + zz * 2
            rows = pl.ds(pl.multiple_of(h * 8, 8), 8)
            dst = rcv.at[pl.ds(pl.multiple_of(me * 8, 8), 8)]
            remote(msg.at[1, rows], dst, a2a_s, a2a_r, (there * 2 + 1, x))

            @pl.when(there != me)
            def _():
                remote(msg.at[0, rows], dst, a2a_s, a2a_r, (there * 2, x))

            @pl.when(there == me)
            def _():
                pltpu.make_async_copy(msg.at[0, rows], dst, a2a_r).start()

            return carry

        lax.fori_loop(0, HEADS, post, 0)

        for p in range(2):
            for d2 in range(2):
                gather_pass(ob, d2, OH, 0, p, o_s, o_r, of_r)
                gather_pass(ob, d2, OH, 1, 1 - p, o_s, o_r, of_r)
        for d2 in range(2):
            for q in range(2):
                gather_last(ob, d2, OH, q, of_r)

        for d2 in range(2):
            for hq in range(NX):
                for j in range(8):
                    hi, lo = split(ob[d2, hq, pl.ds(j, NOUT, stride=8), :])
                    lanes = pl.ds(hq * LANE, LANE)
                    owhl[j, pl.ds(d2 * NOUT, NOUT), lanes] = hi
                    owhl[j, pl.ds(2 * NOUT + d2 * NOUT, NOUT), lanes] = lo

    @pl.when(near)
    def _():
        drain(z1_s, 4 * (7 * R1 + R1 // 2))
        drain(z2_s, 4 * NY * (7 * R2 + R2 // 2))
        straight = 2 * (NZ // 2 - STRAIGHT) + 1
        drain(y_s, (NZ * 2 + straight) * 2 * R1)
        drain(h_s, (NZ - straight) * 2 * R1)
        drain(c_s, NZ * NY * NC * R1)
        drain(c2_s, NZ * NY * NC * R2)
        drain(p_s, 3 * 2 * R2)

    def norm_rows(v):
        m = jnp.sum(v, 0, keepdims=True) / LANE
        q = jnp.sum(v * v, 0, keepdims=True) / LANE - m * m
        return (v - m) * lax.rsqrt(q + EPS)

    @pl.when(even)
    def _():
        wait(rcv, a2a_r)

        def third(s):
            return jnp.concatenate([rcv[pl.ds(2 * s + d2, 64, stride=8), :] for d2 in range(2)], 0)

        kv[c, pl.ds(0, LANE)] = norm_rows(third(1))
        kv[c, pl.ds(LANE, LANE)] = third(2)
        mine = kv.at[c]
        remote(mine, mine, kv_s, kv_r, dev(y, z, 1 - c, x))
        queries = norm_rows(third(0)) * (LANE ** -0.5)
        wait(kv.at[1 - c], kv_r)
        es = []
        for k in range(2):
            keys = kv[k, pl.ds(0, LANE)].T
            es.append(jnp.exp(jnp.dot(keys, queries, precision=HIGHEST, preferred_element_type=F32)))
        norm = jnp.sum(es[0], 0, keepdims=True) + jnp.sum(es[1], 0, keepdims=True)
        o = sum(
            jnp.dot(kv[k, pl.ds(LANE, LANE)], es[k] / norm, precision=HIGHEST, preferred_element_type=F32)
            for k in range(2)
        )
        for d2 in range(2):
            att[0, y, c, pl.ds(d2, 64, stride=2), :] = o[d2 * 64 : d2 * 64 + 64]

    def lies(d, s):
        return place(d, s) // 2

    def b1piece(u, d, s, t):
        n = A1 // PER
        return att.at[lies(d, s - t), y, u // PER, cutting(d, s, u % PER * n, n)]

    def b2piece(u, d, s, t):
        return att.at[lies(d, s - t), pl.ds(u % PER * (NY // PER), NY // PER), u // PER, cutting(d, s, A1, LANE - A1)]

    def b1(u, d, s):
        remote(b1piece(u, d, s, 1), b1piece(u, d, s, 0), z1_s, r1.at[u, d, s - 1], toward[d])

    def b2(u, d, s):
        remote(b2piece(u, d, s, 1), b2piece(u, d, s, 0), z2_s, r2.at[u, d, s - 1], toward[d])

    FIRST = pl.ds(0, A1)
    SECOND = pl.ds(A1, LANE - A1)

    def v1(slot, straight, own=False):
        piece = att.at[slot, y, :, FIRST]
        remote(piece, piece, y_s, ry.at[0, slot], to_yp)
        remote(piece, piece, y_s, ry.at[1, slot], to_ym)
        if straight:
            remote(piece, piece, y_s, rh.at[0, slot], to_yo)
        if not own:
            core(piece, rc.at[slot], c_s)

    def v1pass(slot, straight):
        for q, origin, target in ((0, ym, to_yp), (1, yp, to_ym)):
            wait(att.at[slot, origin, :, FIRST], ry.at[q, slot])
            if not straight:
                piece = att.at[slot, origin, :, ysplit(q, A1)]
                remote(piece, piece, h_s, rh.at[q, slot], target)
        core(att.at[slot, ym, :, FIRST], rc.at[slot], c_s)
        core(att.at[slot, yp, :, FIRST], rc.at[slot], c_s)

    def v1last(slot, straight):
        if straight:
            wait(att.at[slot, yo, :, FIRST], rh.at[0, slot])
        else:
            for q in range(2):
                wait(att.at[slot, yo, :, ysplit(q, A1)], rh.at[q, slot])
        core(att.at[slot, yo, :, FIRST], rc.at[slot], c_s)

    def places(s):
        return [(p, s >= STRAIGHT) for p in sorted({lies(d, s) for d in range(2)})]

    ACROSS = pl.ds(0, 2 * NOUT)

    @pl.when(far)
    def _():
        acc[ACROSS] = jnp.zeros((2 * NOUT, 4 * LANE), F32)

    def finish(p, slot):
        halves = [split(att[p, :, cls].reshape(NY * LANE, LANE)) for cls in range(2)]
        hi = jnp.concatenate([h for h, _ in halves], 1)
        lo = jnp.concatenate([l for _, l in halves], 1)
        acc[ACROSS] += jnp.dot(
            owhl[slot, : 2 * NOUT], jnp.concatenate([hi, lo], 1), preferred_element_type=F32
        )
        acc[ACROSS, : 2 * LANE] += jnp.dot(owhl[slot, 2 * NOUT :], hi, preferred_element_type=F32)

    def round_of(s, before, earlier):
        last = NZ // 2
        for u in range(STREAMS):
            for d in range(2):
                wait(b1piece(u, d, s, 0), r1.at[u, d, s - 1])
                if s < last:
                    b1(u, d, s + 1)
        for place in places(s):
            v1(*place)
        for place in before:
            v1pass(*place)
        for u in range(STREAMS):
            for d in range(2):
                wait(b2piece(u, d, s, 0), r2.at[u, d, s - 1])
                if s < last:
                    b2(u, d, s + 1)
        for slot, _ in places(s):
            core(att.at[slot, :, :, SECOND], rc.at[slot], c_s)
        for place in earlier:
            v1last(*place)

    def last_of(before, earlier):
        for place in before:
            v1pass(*place)
        for place in earlier:
            v1last(*place)

    @pl.when(near & even)
    def _():
        core(att.at[0, y, 1], rc.at[0], c_s)
        wait(att.at[0, y, 0], b_r)
        for u in range(STREAMS):
            for d in range(2):
                b1(u, d, 1)
        own = att.at[0, y, :, SECOND]
        for k, target in enumerate((to_yp, to_ym, to_yo)):
            remote(own, own, p_s, rp.at[k], target)
        v1(0, False, True)
        for k, origin in enumerate((ym, yp, yo)):
            wait(att.at[0, origin, :, SECOND], rp.at[k])
        for u in range(STREAMS):
            for d in range(2):
                b2(u, d, 1)
        for origin in (ym, yp, yo):
            core(att.at[0, origin, :, SECOND], rc.at[0], c_s)
        round_of(2, places(0), [])
        round_of(4, places(2), places(0))
        round_of(6, places(4), places(2))
        round_of(8, places(6), places(4))
        last_of(places(8), places(6) + places(8))

    @pl.when(near & odd)
    def _():
        round_of(1, [], [])
        round_of(3, places(1), [])
        round_of(5, places(3), places(1))
        round_of(7, places(5), places(3))
        last_of(places(7), places(5) + places(7))

    def from_near(s):
        for d in range(1 if s in (0, NZ // 2) else 2):
            p = lies(d, s)
            if s:
                wait(att.at[p], rc.at[p])
            else:
                drain(rc.at[p], (2 * NY - 1) * LANE)
            finish(p, back(d, s) // 2)

    @pl.when(far & even)
    def _():
        own = att.at[0, y, 0]
        remote(own, own, b_s, b_r, dev(y, z, 1, x))
        for s in (0, 2, 4, 6, 8):
            from_near(s)
        wait(own, b_s)

    @pl.when(far & odd)
    def _():
        for s in (1, 3, 5, 7):
            from_near(s)

    @pl.when(far)
    def _():
        sums = acc[ACROSS, : 2 * LANE] + acc[ACROSS, 2 * LANE :]
        for k in range(2):
            mine = sums[:, k * LANE : (k + 1) * LANE]
            turn[pl.ds(k * LANE, LANE)] = jnp.concatenate([mine, jnp.zeros((LANE - 2 * NOUT, LANE), F32)], 0).T
        for q in range(NX):
            for cls in range(NC):
                mine = turn[pl.ds(q * NC + cls, 2 * NZ, stride=NY * NC), :]
                for cc in range(NC):
                    fs[q, cc, pl.ds(cls * 32, 32), pl.ds(0, NOUT)] = mine[:, cc * NOUT : cc * NOUT + NOUT]
        for dx in (2, 1, 3, 0):
            for cc in range(NC):
                if dx or cc:
                    tx = (x + dx) % NX
                    remote(fs.at[tx, cc], fr.at[x], f_s, f_r.at[dx], dev(y, z, cc, tx))
        fr[x] = fs[x, 0]

    @pl.when(near)
    def _():
        wait(fr.at[0], f_r.at[0])

    for dx in range(1, NX):
        wait(fr.at[0], f_r.at[dx])
    for i in range(NX):
        for cls in range(NC):
            for b in range(2):
                out[i, pl.ds(2 * cls + b, 16, stride=4), :] = fr[i, pl.ds(cls * 32 + b, 16, stride=2), :][:, :NOUT]

    for i in range(1, NX):
        wait(chunk.at[0, 0], act_s.at[i])

    @pl.when(even)
    def _():
        wait(kv.at[0], kv_s)

    @pl.when(far)
    def _():
        wait(chunk.at[0, 0], act_s.at[0])
        drain(w_s, 12 * WH)
        drain(o_s, 12 * OH)
        drain(f_s, 7 * 64)

    @pl.when(far & even)
    def _():
        drain(a2a_s, (2 * HEADS - 1) * 8)

    @pl.when(far & odd)
    def _():
        drain(a2a_s, 2 * HEADS * 8)

    @pl.when(near)
    def _():
        drain(wn_s, 2 * WH)
        drain(on_s, 2 * OH)

    @pl.when(near & even)
    def _():
        drain(z1_s, 2 * NC * 4 * A1)
        drain(z2_s, 2 * NC * 4 * NY * (LANE - A1))
        drain(y_s, (NZZ * 2 + 1) * 2 * A1)
        drain(h_s, (NZZ - 1) * 2 * A1)
        drain(c_s, NZZ * NY * NC * LANE - LANE)
        drain(p_s, 3 * 2 * (LANE - A1))

    @pl.when(near & odd)
    def _():
        drain(z1_s, NC * 7 * A1)
        drain(z2_s, NC * 7 * NY * (LANE - A1))
        drain(y_s, (NZZ * 2 + 2) * 2 * A1)
        drain(h_s, (NZZ - 2) * 2 * A1)
        drain(c_s, NZZ * NY * NC * LANE)


def shards(activations, input_weight, output_weight):
    w = input_weight.reshape(FEAT * KT, LANE)
    ow = output_weight.reshape(NOUT * 8, LANE)
    dma = pltpu.SemaphoreType.DMA
    vm = pltpu.VMEM
    scratch = [
        vm((NC, NX, 2, KT * LANE), F32),
        vm((NZ, NY, NC, R, LANE), F32),
        vm((NC, NX, FEAT * KT, LANE), F32),
        vm((NX, 4 * FEAT, KT * LANE), BF16),
        vm((NX, 4 * LANE, KT * LANE), BF16),
        vm((NC, NX, NOUT * 8, LANE), F32),
        vm((NZZ, 4 * NOUT, NY * LANE), BF16),
        vm((NC, HEADS * 8, LANE), F32),
        vm((NY * NZ * 8, LANE), F32),
        vm((NC, 2 * LANE, LANE), F32),
        vm((NZZ, NY, NC, LANE, LANE), F32),
        vm((NX, NC, 64, LANE), F32),
        vm((NX, 64, LANE), F32),
        vm((2 * LANE, LANE), F32),
        vm((2 * FEAT, 4 * LANE), F32),
        dma((NX,)), dma((NC, NX)),
        dma, dma((2, 2, 2)), dma((2, 2)), dma, dma,
        dma, dma((2, 2, 2)), dma((2, 2)), dma, dma,
        dma, dma, dma, dma, dma, dma, dma,
        dma((STREAMS, 2, 8)), dma((STREAMS, 2, 8)),
        dma((2, NZ)), dma((2, NZ)), dma((3,)),
        dma((NZ,)),
        dma, dma, dma, dma, dma, dma,
        dma, dma((NX,)),
        dma((2,)),
    ]
    return pl.pallas_call(
        kernel,
        out_shape=jax.ShapeDtypeStruct((NX, 64, NOUT), F32),
        in_specs=[
            pl.BlockSpec(memory_space=pl.ANY),
            pl.BlockSpec(memory_space=pl.ANY),
            pl.BlockSpec(memory_space=pl.ANY),
        ],
        out_specs=pl.BlockSpec(memory_space=pltpu.VMEM),
        scratch_shapes=scratch,
        compiler_params=pltpu.CompilerParams(
            collective_id=0, has_side_effects=True, vmem_limit_bytes=60 * 1024 * 1024
        ),
    )(activations, w, ow)


def solution(mesh):
    return jax.shard_map(
        shards,
        mesh=mesh,
        in_specs=(P(None, "row", "col"), P(None, None, "row", "col"), P("row", "col", None)),
        out_specs=P(None, "col", "row"),
        check_vma=False,
    )
```

```python
import jax
import jax.numpy as jnp
from jax import lax
from jax.experimental import pallas as pl
from jax.experimental.pallas import tpu as pltpu
from jax.sharding import PartitionSpec as P

MESH = pl.DeviceIdType.MESH
EPS = 1e-06
HIGHEST = lax.Precision.HIGHEST
F32 = jnp.float32
BF16 = jnp.bfloat16

NX, NY, NZ, NC = 4, 4, 16, 2
LANE = 128
TILES = 48
KT = TILES // NX
R = 2 * TILES
R1, R2 = 72, 24
STRAIGHT = 7
STREAMS = 2
PER = STREAMS // 2
HEADS = 32
NZZ = 8
A1 = 104
FEAT = 96
NOUT = 48


def split(x):
    hi = x.astype(BF16)
    return hi, (x - hi.astype(F32)).astype(BF16)


def kernel(act, w, ow, out, *scratch):
    (chunk, g, wb, whl, ghl, ob, owhl, msg, rcv, kv, att, fs, fr, turn, acc,
     act_s, act_r, w_s, w_r, wf_r, wn_s, wn_r, o_s, o_r, of_r, on_s, on_r,
     z1_s, z2_s, y_s, h_s, c_s, c2_s, p_s, r1, r2, ry, rh, rp, rc,
     a2a_s, a2a_r, kv_s, kv_r, b_s, b_r, f_s, f_r, loc) = scratch
    row = lax.axis_index("row")
    x = lax.axis_index("col")
    c = row % 2
    z = row // 2 % NZ
    y = row // (2 * NZ)
    me = y * NZ + z
    near, far = c == 1, c == 0
    even, odd = z % 2 == 0, z % 2 == 1

    def dev(yy, zz, cc, xx):
        return ((yy * NZ + zz) * 2 + cc, xx)

    def wrap(v, n):
        return (v + n) % n

    def remote(src, dst, ssem, rsem, where):
        pltpu.make_async_remote_copy(
            src_ref=src, dst_ref=dst, send_sem=ssem, recv_sem=rsem, device_id=where, device_id_type=MESH
        ).start()

    def wait(ref, sem):
        pltpu.make_async_copy(ref, ref, sem).wait()

    flat = wb.reshape(NC * NX * FEAT * KT, LANE)

    def drain(sem, rows):
        wait(flat.at[pl.ds(0, rows)], sem)

    xp, xm, xo = wrap(x + 1, NX), wrap(x - 1, NX), wrap(x + 2, NX)
    yp, ym, yo = wrap(y + 1, NY), wrap(y - 1, NY), wrap(y + 2, NY)

    bar = pltpu.get_barrier_semaphore()

    def greet(where):
        pl.semaphore_signal(bar, inc=1, device_id=where, device_id_type=MESH)

    @pl.when(near)
    def _():
        greet(dev(y, z, 0, x))
        for i in range(1, NX):
            for cc in range(NC):
                greet(dev(y, z, cc, wrap(x + i, NX)))
        for dz in (1, -1):
            greet(dev(y, wrap(z + dz, NZ), 1, x))
        for yy in (yp, ym, yo):
            greet(dev(yy, z, 1, x))
        pl.semaphore_wait(bar, 1 + NX - 1 + 2 + NY - 1)

    @pl.when(far)
    def _():
        greet(dev(y, z, 1, x))
        for xx in (xp, xm):
            greet(dev(y, z, 0, xx))
        pl.semaphore_wait(bar, NX + 2)

    for i in range(1, NX):
        xt = (x + i) % NX
        remote(act.at[xt], chunk.at[c, x], act_s.at[i], act_r.at[c, i], dev(y, z, 1, xt))

    @pl.when(far)
    def _():
        remote(act.at[x], chunk.at[0, x], act_s.at[0], act_r.at[0, 0], dev(y, z, 1, x))

    @pl.when(near)
    def _():
        pltpu.make_async_copy(act.at[x], chunk.at[1, x], act_r.at[1, 0]).start()
        remote(w, wb.at[1, x], wn_s, wn_r, dev(y, z, 0, x))
        remote(ow, ob.at[1, x], on_s, on_r, dev(y, z, 0, x))

    def gather_send(src, buf, d2, half, ss, rs):
        for q, (first, target) in enumerate(((0, xp), (1, xm))):
            for p in (first, 1 - first):
                rows = pl.ds(p * half, half)
                remote(src.at[rows], buf.at[d2, x, rows], ss, rs.at[d2, q, p], dev(y, z, 0, target))

    def gather_pass(buf, d2, half, q, p, ss, rs, fr_):
        origin = xm if q == 0 else xp
        piece = buf.at[d2, origin, pl.ds(p * half, half)]
        wait(piece, rs.at[d2, q, p])
        if p == q:
            remote(piece, piece, ss, fr_.at[d2, q], dev(y, z, 0, xp if q == 0 else xm))

    def gather_last(buf, d2, half, q, fr_):
        wait(buf.at[d2, xo, pl.ds(q * half, half)], fr_.at[d2, q])

    WH = FEAT * KT // 2
    OH = NOUT * 8 // 2

    def wconv(d2, origin, p):
        def body(kt, carry):
            v = wb[d2, origin, pl.ds(p * WH + kt, FEAT // 2, stride=KT), :]
            hi, lo = split(v)
            lanes = pl.ds(pl.multiple_of(kt * LANE, LANE), LANE)
            at = d2 * FEAT + p * (FEAT // 2)
            whl[origin, pl.ds(at, FEAT // 2), lanes] = hi
            whl[origin, pl.ds(at + 2 * FEAT, FEAT // 2), lanes] = lo
            return carry

        lax.fori_loop(0, KT, body, 0)

    def ysplit(q, n):
        share = (n // 2 + 7) // 8 * 8
        return pl.ds(share, n - share) if q else pl.ds(0, share)

    def core(piece, sem, sent):
        remote(piece, piece, sent, sem, to_far)

    def place(d, s):
        return (NZ - s) % NZ if d else s

    def back(d, s):
        return wrap(z - s, NZ) if d == 0 else wrap(z + s, NZ)

    toward = [dev(y, wrap(z + 1, NZ), 1, x), dev(y, wrap(z - 1, NZ), 1, x)]
    to_yp, to_ym, to_yo = [dev(yy, z, 1, x) for yy in (yp, ym, yo)]
    to_far = dev(y, z, 0, x)

    ONES = pl.ds(0, R1)
    TWOS = pl.ds(R1, R2)

    def cutting(d, s, first, n):
        if s < NZ // 2:
            return pl.ds(first, n)
        share = (n // 2 + 7) // 8 * 8
        return pl.ds(first + share, n - share) if d else pl.ds(first, share)

    def z1piece(u, d, s, t):
        n = R1 // PER
        return g.at[place(d, s - t), y, u // PER, cutting(d, s, u % PER * n, n)]

    def z2piece(u, d, s, t):
        return g.at[place(d, s - t), pl.ds(u % PER * (NY // PER), NY // PER), u // PER, cutting(d, s, R1, R2)]

    def z1(u, d, s):
        remote(z1piece(u, d, s, 1), z1piece(u, d, s, 0), z1_s, r1.at[u, d, s - 1], toward[d])

    def z2(u, d, s):
        remote(z2piece(u, d, s, 1), z2piece(u, d, s, 0), z2_s, r2.at[u, d, s - 1], toward[d])

    def y1(slot, straight):
        piece = g.at[slot, y, :, ONES]
        remote(piece, piece, y_s, ry.at[0, slot], to_yp)
        remote(piece, piece, y_s, ry.at[1, slot], to_ym)
        if straight:
            remote(piece, piece, y_s, rh.at[0, slot], to_yo)
        core(piece, rc.at[slot], c_s)

    def y1pass(slot, straight):
        for q, origin, target in ((0, ym, to_yp), (1, yp, to_ym)):
            wait(g.at[slot, origin, :, ONES], ry.at[q, slot])
            if not straight:
                piece = g.at[slot, origin, :, ysplit(q, R1)]
                remote(piece, piece, h_s, rh.at[q, slot], target)
        core(g.at[slot, ym, :, ONES], rc.at[slot], c_s)
        core(g.at[slot, yp, :, ONES], rc.at[slot], c_s)

    def y1last(slot, straight):
        if straight:
            wait(g.at[slot, yo, :, ONES], rh.at[0, slot])
        else:
            for q in range(2):
                wait(g.at[slot, yo, :, ysplit(q, R1)], rh.at[q, slot])
        core(g.at[slot, yo, :, ONES], rc.at[slot], c_s)

    def spots(s):
        return [(p, s >= STRAIGHT) for p in sorted({place(d, s) for d in range(2)})]

    @pl.when(near)
    def _():
        for cls in range(2):
            for i in range(NX):
                wait(chunk.at[0, 0], act_r.at[cls, i])
        for cls in range(2):
            data = chunk[cls]
            width = TILES * LANE

            def mean(v):
                return jnp.sum(jnp.sum(v, 0, keepdims=True), 2, keepdims=True) / width

            center = mean(data)
            scale = lax.rsqrt(mean(data * data) - center * center + EPS)
            normed = (data - center) * scale
            for t in range(TILES):
                v = normed[t // KT, :, t % KT * LANE : (t % KT + 1) * LANE]
                g[0, y, cls, pl.ds(2 * t, 2), :] = v
            for u in range(PER * cls, PER * cls + PER):
                for d in range(2):
                    z1(u, d, 1)
        own2 = g.at[0, y, :, TWOS]
        for k, target in enumerate((to_yp, to_ym, to_yo)):
            remote(own2, own2, p_s, rp.at[k], target)
        y1(0, False)
        for k, origin in enumerate((ym, yp, yo)):
            wait(g.at[0, origin, :, TWOS], rp.at[k])
        for u in range(STREAMS):
            for d in range(2):
                z2(u, d, 1)
        core(g.at[0, :, :, TWOS], rc.at[0], c2_s)
        last = NZ // 2
        for s in range(1, last + 3):
            if s <= last:
                for u in range(STREAMS):
                    for d in range(2):
                        wait(z1piece(u, d, s, 0), r1.at[u, d, s - 1])
                        if s < last:
                            z1(u, d, s + 1)
                for spot in spots(s):
                    y1(*spot)
            t = s - 1
            if 1 <= t <= last:
                for u in range(STREAMS):
                    for d in range(2):
                        wait(z2piece(u, d, t, 0), r2.at[u, d, t - 1])
                        if t < last:
                            z2(u, d, t + 1)
                for slot, _ in spots(t):
                    core(g.at[slot, :, :, TWOS], rc.at[slot], c2_s)
            if 0 <= s - 1 <= last:
                for spot in spots(s - 1):
                    y1pass(*spot)
            if 0 <= s - 2 <= last:
                for spot in spots(s - 2):
                    y1last(*spot)

    @pl.when(far)
    def _():
        own = pltpu.make_async_copy(w, wb.at[0, x], loc.at[0])
        own.start()
        gather_send(w, wb, 0, WH, w_s, w_r)
        wait(wb.at[1, x], wn_r)
        gather_send(wb.at[1, x], wb, 1, WH, w_s, w_r)
        own.wait()
        for d2 in range(2):
            for p in range(2):
                wconv(d2, x, p)
        for p in range(2):
            for d2 in range(2):
                gather_pass(wb, d2, WH, 0, p, w_s, w_r, wf_r)
                gather_pass(wb, d2, WH, 1, 1 - p, w_s, w_r, wf_r)
            for d2 in range(2):
                wconv(d2, xm, p)
                wconv(d2, xp, 1 - p)
        own = pltpu.make_async_copy(ow, ob.at[0, x], loc.at[1])
        own.start()
        gather_send(ow, ob, 0, OH, o_s, o_r)
        wait(ob.at[1, x], on_r)
        gather_send(ob.at[1, x], ob, 1, OH, o_s, o_r)
        for d2 in range(2):
            for q in range(2):
                gather_last(wb, d2, WH, q, wf_r)
                wconv(d2, xo, q)
        own.wait()

        flat_g = g.reshape(NZ * NY * NC * R, LANE)

        def arrive(k, carry):
            away = (k + 1) // 2
            lies = away + (NZ - 2 * away) * (k % 2)
            slot = wrap(z - away + 2 * away * (k % 2), NZ)
            wait(g.at[lies], rc.at[lies])
            rows = pl.ds(pl.multiple_of(slot * 16, 16), 16)
            low = pl.ds(pl.multiple_of(2 * LANE + slot * 16, 16), 16)
            for t in range(TILES):
                v = jnp.concatenate(
                    [flat_g[pl.ds(lies * (NY * NC * R) + 2 * t + b, NY * NC, stride=R), :] for b in range(2)], 0
                )
                hi, lo = split(v)
                lanes = pl.ds(t % KT * LANE, LANE)
                ghl[t // KT, rows, lanes] = hi
                ghl[t // KT, low, lanes] = lo
            return carry

        lax.fori_loop(0, NZ, arrive, 0)

        acc[...] = jnp.zeros_like(acc)
        turned = (((1,), (1,)), ((), ()))

        def project(k, carry):
            acc[...] += lax.dot_general(whl[k, : 2 * FEAT], ghl[k], turned, preferred_element_type=F32)
            acc[:, :256] += lax.dot_general(
                whl[k, 2 * FEAT :], ghl[k, :256], turned, preferred_element_type=F32
            )
            return carry

        lax.fori_loop(0, NX, project, 0)
        triples = acc[:, :256] + acc[:, 256:]

        msg[...] = jnp.zeros_like(msg)
        for cls in range(2):
            for d2 in range(2):
                for s in range(3):
                    at = d2 * FEAT + s * HEADS
                    msg[cls, pl.ds(2 * s + d2, HEADS, stride=8), :] = triples[
                        at : at + HEADS, cls * LANE : (cls + 1) * LANE
                    ]

        def post(k, carry):
            j = k // NY
            zz = (z // 2 + 4 + (j + 1) // 2 * (1 - 2 * (j % 2))) % NZZ
            yy = (y + 2 + k) % NY
            h = yy * NZZ + zz
            there = yy * NZ + zz * 2
            rows = pl.ds(pl.multiple_of(h * 8, 8), 8)
            dst = rcv.at[pl.ds(pl.multiple_of(me * 8, 8), 8)]
            remote(msg.at[1, rows], dst, a2a_s, a2a_r, (there * 2 + 1, x))

            @pl.when(there != me)
            def _():
                remote(msg.at[0, rows], dst, a2a_s, a2a_r, (there * 2, x))

            @pl.when(there == me)
            def _():
                pltpu.make_async_copy(msg.at[0, rows], dst, a2a_r).start()

            return carry

        lax.fori_loop(0, HEADS, post, 0)

        for p in range(2):
            for d2 in range(2):
                gather_pass(ob, d2, OH, 0, p, o_s, o_r, of_r)
                gather_pass(ob, d2, OH, 1, 1 - p, o_s, o_r, of_r)
        for d2 in range(2):
            for q in range(2):
                gather_last(ob, d2, OH, q, of_r)

        for d2 in range(2):
            for hq in range(NX):
                for j in range(8):
                    hi, lo = split(ob[d2, hq, pl.ds(j, NOUT, stride=8), :])
                    lanes = pl.ds(hq * LANE, LANE)
                    owhl[j, pl.ds(d2 * NOUT, NOUT), lanes] = hi
                    owhl[j, pl.ds(2 * NOUT + d2 * NOUT, NOUT), lanes] = lo

    @pl.when(near)
    def _():
        drain(z1_s, 4 * (7 * R1 + R1 // 2))
        drain(z2_s, 4 * NY * (7 * R2 + R2 // 2))
        straight = 2 * (NZ // 2 - STRAIGHT) + 1
        drain(y_s, (NZ * 2 + straight) * 2 * R1)
        drain(h_s, (NZ - straight) * 2 * R1)
        drain(c_s, NZ * NY * NC * R1)
        drain(c2_s, NZ * NY * NC * R2)
        drain(p_s, 3 * 2 * R2)

    def norm_rows(v):
        m = jnp.sum(v, 0, keepdims=True) / LANE
        q = jnp.sum(v * v, 0, keepdims=True) / LANE - m * m
        return (v - m) * lax.rsqrt(q + EPS)

    @pl.when(even)
    def _():
        wait(rcv, a2a_r)

        def third(s):
            return jnp.concatenate([rcv[pl.ds(2 * s + d2, 64, stride=8), :] for d2 in range(2)], 0)

        kv[c, pl.ds(0, LANE)] = norm_rows(third(1))
        kv[c, pl.ds(LANE, LANE)] = third(2)
        mine = kv.at[c]
        remote(mine, mine, kv_s, kv_r, dev(y, z, 1 - c, x))
        queries = norm_rows(third(0)) * (LANE ** -0.5)
        wait(kv.at[1 - c], kv_r)
        es = []
        for k in range(2):
            keys = kv[k, pl.ds(0, LANE)].T
            es.append(jnp.exp(jnp.dot(keys, queries, precision=HIGHEST, preferred_element_type=F32)))
        norm = jnp.sum(es[0], 0, keepdims=True) + jnp.sum(es[1], 0, keepdims=True)
        o = sum(
            jnp.dot(kv[k, pl.ds(LANE, LANE)], es[k] / norm, precision=HIGHEST, preferred_element_type=F32)
            for k in range(2)
        )
        for d2 in range(2):
            att[0, y, c, pl.ds(d2, 64, stride=2), :] = o[d2 * 64 : d2 * 64 + 64]

    def lies(d, s):
        return place(d, s) // 2

    def b1piece(u, d, s, t):
        n = A1 // PER
        return att.at[lies(d, s - t), y, u // PER, cutting(d, s, u % PER * n, n)]

    def b2piece(u, d, s, t):
        return att.at[lies(d, s - t), pl.ds(u % PER * (NY // PER), NY // PER), u // PER, cutting(d, s, A1, LANE - A1)]

    def b1(u, d, s):
        remote(b1piece(u, d, s, 1), b1piece(u, d, s, 0), z1_s, r1.at[u, d, s - 1], toward[d])

    def b2(u, d, s):
        remote(b2piece(u, d, s, 1), b2piece(u, d, s, 0), z2_s, r2.at[u, d, s - 1], toward[d])

    FIRST = pl.ds(0, A1)
    SECOND = pl.ds(A1, LANE - A1)

    def v1(slot, straight, own=False):
        piece = att.at[slot, y, :, FIRST]
        remote(piece, piece, y_s, ry.at[0, slot], to_yp)
        remote(piece, piece, y_s, ry.at[1, slot], to_ym)
        if straight:
            remote(piece, piece, y_s, rh.at[0, slot], to_yo)
        if not own:
            core(piece, rc.at[slot], c_s)

    def v1pass(slot, straight):
        for q, origin, target in ((0, ym, to_yp), (1, yp, to_ym)):
            wait(att.at[slot, origin, :, FIRST], ry.at[q, slot])
            if not straight:
                piece = att.at[slot, origin, :, ysplit(q, A1)]
                remote(piece, piece, h_s, rh.at[q, slot], target)
        core(att.at[slot, ym, :, FIRST], rc.at[slot], c_s)
        core(att.at[slot, yp, :, FIRST], rc.at[slot], c_s)

    def v1last(slot, straight):
        if straight:
            wait(att.at[slot, yo, :, FIRST], rh.at[0, slot])
        else:
            for q in range(2):
                wait(att.at[slot, yo, :, ysplit(q, A1)], rh.at[q, slot])
        core(att.at[slot, yo, :, FIRST], rc.at[slot], c_s)

    def places(s):
        return [(p, s >= STRAIGHT) for p in sorted({lies(d, s) for d in range(2)})]

    ACROSS = pl.ds(0, 2 * NOUT)

    @pl.when(far)
    def _():
        acc[ACROSS] = jnp.zeros((2 * NOUT, 4 * LANE), F32)

    def finish(p, slot):
        halves = [split(att[p, :, cls].reshape(NY * LANE, LANE)) for cls in range(2)]
        hi = jnp.concatenate([h for h, _ in halves], 1)
        lo = jnp.concatenate([l for _, l in halves], 1)
        acc[ACROSS] += jnp.dot(
            owhl[slot, : 2 * NOUT], jnp.concatenate([hi, lo], 1), preferred_element_type=F32
        )
        acc[ACROSS, : 2 * LANE] += jnp.dot(owhl[slot, 2 * NOUT :], hi, preferred_element_type=F32)

    def round_of(s, before, earlier):
        last = NZ // 2
        for u in range(STREAMS):
            for d in range(2):
                wait(b1piece(u, d, s, 0), r1.at[u, d, s - 1])
                if s < last:
                    b1(u, d, s + 1)
        for place in places(s):
            v1(*place)
        for place in before:
            v1pass(*place)
        for u in range(STREAMS):
            for d in range(2):
                wait(b2piece(u, d, s, 0), r2.at[u, d, s - 1])
                if s < last:
                    b2(u, d, s + 1)
        for slot, _ in places(s):
            core(att.at[slot, :, :, SECOND], rc.at[slot], c_s)
        for place in earlier:
            v1last(*place)

    def last_of(before, earlier):
        for place in before:
            v1pass(*place)
        for place in earlier:
            v1last(*place)

    @pl.when(near & even)
    def _():
        core(att.at[0, y, 1], rc.at[0], c_s)
        wait(att.at[0, y, 0], b_r)
        for u in range(STREAMS):
            for d in range(2):
                b1(u, d, 1)
        own = att.at[0, y, :, SECOND]
        for k, target in enumerate((to_yp, to_ym, to_yo)):
            remote(own, own, p_s, rp.at[k], target)
        v1(0, False, True)
        for k, origin in enumerate((ym, yp, yo)):
            wait(att.at[0, origin, :, SECOND], rp.at[k])
        for u in range(STREAMS):
            for d in range(2):
                b2(u, d, 1)
        for origin in (ym, yp, yo):
            core(att.at[0, origin, :, SECOND], rc.at[0], c_s)
        round_of(2, places(0), [])
        round_of(4, places(2), places(0))
        round_of(6, places(4), places(2))
        round_of(8, places(6), places(4))
        last_of(places(8), places(6) + places(8))

    @pl.when(near & odd)
    def _():
        round_of(1, [], [])
        round_of(3, places(1), [])
        round_of(5, places(3), places(1))
        round_of(7, places(5), places(3))
        last_of(places(7), places(5) + places(7))

    def from_near(s):
        for d in range(1 if s in (0, NZ // 2) else 2):
            p = lies(d, s)
            if s:
                wait(att.at[p], rc.at[p])
            else:
                drain(rc.at[p], (2 * NY - 1) * LANE)
            finish(p, back(d, s) // 2)

    @pl.when(far & even)
    def _():
        own = att.at[0, y, 0]
        remote(own, own, b_s, b_r, dev(y, z, 1, x))
        for s in (0, 2, 4, 6, 8):
            from_near(s)
        wait(own, b_s)

    @pl.when(far & odd)
    def _():
        for s in (1, 3, 5, 7):
            from_near(s)

    @pl.when(far)
    def _():
        sums = acc[ACROSS, : 2 * LANE] + acc[ACROSS, 2 * LANE :]
        for k in range(2):
            mine = sums[:, k * LANE : (k + 1) * LANE]
            turn[pl.ds(k * LANE, LANE)] = jnp.concatenate([mine, jnp.zeros((LANE - 2 * NOUT, LANE), F32)], 0).T
        for q in range(NX):
            for cls in range(NC):
                mine = turn[pl.ds(q * NC + cls, 2 * NZ, stride=NY * NC), :]
                for cc in range(NC):
                    fs[q, cc, pl.ds(cls * 32, 32), pl.ds(0, NOUT)] = mine[:, cc * NOUT : cc * NOUT + NOUT]
        for dx in (2, 1, 3, 0):
            for cc in range(NC):
                if dx or cc:
                    tx = (x + dx) % NX
                    remote(fs.at[tx, cc], fr.at[x], f_s, f_r.at[dx], dev(y, z, cc, tx))
        fr[x] = fs[x, 0]

    @pl.when(near)
    def _():
        wait(fr.at[0], f_r.at[0])

    for dx in range(1, NX):
        wait(fr.at[0], f_r.at[dx])
    for i in range(NX):
        for cls in range(NC):
            for b in range(2):
                out[i, pl.ds(2 * cls + b, 16, stride=4), :] = fr[i, pl.ds(cls * 32 + b, 16, stride=2), :][:, :NOUT]

    for i in range(1, NX):
        wait(chunk.at[0, 0], act_s.at[i])

    @pl.when(even)
    def _():
        wait(kv.at[0], kv_s)

    @pl.when(far)
    def _():
        wait(chunk.at[0, 0], act_s.at[0])
        drain(w_s, 12 * WH)
        drain(o_s, 12 * OH)
        drain(f_s, 7 * 64)

    @pl.when(far & even)
    def _():
        drain(a2a_s, (2 * HEADS - 1) * 8)

    @pl.when(far & odd)
    def _():
        drain(a2a_s, 2 * HEADS * 8)

    @pl.when(near)
    def _():
        drain(wn_s, 2 * WH)
        drain(on_s, 2 * OH)

    @pl.when(near & even)
    def _():
        drain(z1_s, 2 * NC * 4 * A1)
        drain(z2_s, 2 * NC * 4 * NY * (LANE - A1))
        drain(y_s, (NZZ * 2 + 1) * 2 * A1)
        drain(h_s, (NZZ - 1) * 2 * A1)
        drain(c_s, NZZ * NY * NC * LANE - LANE)
        drain(p_s, 3 * 2 * (LANE - A1))

    @pl.when(near & odd)
    def _():
        drain(z1_s, NC * 7 * A1)
        drain(z2_s, NC * 7 * NY * (LANE - A1))
        drain(y_s, (NZZ * 2 + 2) * 2 * A1)
        drain(h_s, (NZZ - 2) * 2 * A1)
        drain(c_s, NZZ * NY * NC * LANE)


def shards(activations, input_weight, output_weight):
    w = input_weight.reshape(FEAT * KT, LANE)
    ow = output_weight.reshape(NOUT * 8, LANE)
    dma = pltpu.SemaphoreType.DMA
    vm = pltpu.VMEM
    scratch = [
        vm((NC, NX, 2, KT * LANE), F32),
        vm((NZ, NY, NC, R, LANE), F32),
        vm((NC, NX, FEAT * KT, LANE), F32),
        vm((NX, 4 * FEAT, KT * LANE), BF16),
        vm((NX, 4 * LANE, KT * LANE), BF16),
        vm((NC, NX, NOUT * 8, LANE), F32),
        vm((NZZ, 4 * NOUT, NY * LANE), BF16),
        vm((NC, HEADS * 8, LANE), F32),
        vm((NY * NZ * 8, LANE), F32),
        vm((NC, 2 * LANE, LANE), F32),
        vm((NZZ, NY, NC, LANE, LANE), F32),
        vm((NX, NC, 64, LANE), F32),
        vm((NX, 64, LANE), F32),
        vm((2 * LANE, LANE), F32),
        vm((2 * FEAT, 4 * LANE), F32),
        dma((NX,)), dma((NC, NX)),
        dma, dma((2, 2, 2)), dma((2, 2)), dma, dma,
        dma, dma((2, 2, 2)), dma((2, 2)), dma, dma,
        dma, dma, dma, dma, dma, dma, dma,
        dma((STREAMS, 2, 8)), dma((STREAMS, 2, 8)),
        dma((2, NZ)), dma((2, NZ)), dma((3,)),
        dma((NZ,)),
        dma, dma, dma, dma, dma, dma,
        dma, dma((NX,)),
        dma((2,)),
    ]
    return pl.pallas_call(
        kernel,
        out_shape=jax.ShapeDtypeStruct((NX, 64, NOUT), F32),
        in_specs=[
            pl.BlockSpec(memory_space=pl.ANY),
            pl.BlockSpec(memory_space=pl.ANY),
            pl.BlockSpec(memory_space=pl.ANY),
        ],
        out_specs=pl.BlockSpec(memory_space=pltpu.VMEM),
        scratch_shapes=scratch,
        compiler_params=pltpu.CompilerParams(
            collective_id=0, has_side_effects=True, vmem_limit_bytes=60 * 1024 * 1024
        ),
    )(activations, w, ow)


def solution(mesh):
    return jax.shard_map(
        shards,
        mesh=mesh,
        in_specs=(P(None, "row", "col"), P(None, None, "row", "col"), P("row", "col", None)),
        out_specs=P(None, "col", "row"),
        check_vma=False,
    )
```

```python
import jax
import jax.numpy as jnp
from jax import lax
from jax.experimental import pallas as pl
from jax.experimental.pallas import tpu as pltpu
from jax.sharding import PartitionSpec as P

MESH = pl.DeviceIdType.MESH
EPS = 1e-06
HIGHEST = lax.Precision.HIGHEST
F32 = jnp.float32
BF16 = jnp.bfloat16

NX, NY, NZ, NC = 4, 4, 16, 2
LANE = 128
TILES = 48
KT = TILES // NX
R = 2 * TILES
R1, R2 = 72, 24
STRAIGHT = 7
STREAMS = 2
PER = STREAMS // 2
EARLY = 9
HEADS = 32
NZZ = 8
A1 = 104
FEAT = 96
NOUT = 48


def split(x):
    hi = x.astype(BF16)
    return hi, (x - hi.astype(F32)).astype(BF16)


def kernel(act, w, ow, out, *scratch):
    (chunk, g, wb, whl, ghl, ob, owhl, msg, rcv, kv, att, fs, fr, turn, acc,
     act_s, act_r, w_s, w_r, wf_r, wn_s, wn_r, o_s, o_r, of_r, on_s, on_r,
     z1_s, z2_s, y_s, h_s, c_s, c2_s, p_s, r1, r2, ry, rh, rp, rc,
     a2a_s, a2a_r, kv_s, kv_r, b_s, b_r, f_s, f_r, loc) = scratch
    row = lax.axis_index("row")
    x = lax.axis_index("col")
    c = row % 2
    z = row // 2 % NZ
    y = row // (2 * NZ)
    me = y * NZ + z
    near, far = c == 1, c == 0
    even, odd = z % 2 == 0, z % 2 == 1

    def dev(yy, zz, cc, xx):
        return ((yy * NZ + zz) * 2 + cc, xx)

    def wrap(v, n):
        return (v + n) % n

    def remote(src, dst, ssem, rsem, where):
        pltpu.make_async_remote_copy(
            src_ref=src, dst_ref=dst, send_sem=ssem, recv_sem=rsem, device_id=where, device_id_type=MESH
        ).start()

    def wait(ref, sem):
        pltpu.make_async_copy(ref, ref, sem).wait()

    flat = wb.reshape(NC * NX * FEAT * KT, LANE)

    def drain(sem, rows):
        wait(flat.at[pl.ds(0, rows)], sem)

    xp, xm, xo = wrap(x + 1, NX), wrap(x - 1, NX), wrap(x + 2, NX)
    yp, ym, yo = wrap(y + 1, NY), wrap(y - 1, NY), wrap(y + 2, NY)

    bar = pltpu.get_barrier_semaphore()

    def greet(where):
        pl.semaphore_signal(bar, inc=1, device_id=where, device_id_type=MESH)

    @pl.when(near)
    def _():
        greet(dev(y, z, 0, x))
        for i in range(1, NX):
            for cc in range(NC):
                greet(dev(y, z, cc, wrap(x + i, NX)))
        for dz in (1, -1):
            greet(dev(y, wrap(z + dz, NZ), 1, x))
        for yy in (yp, ym, yo):
            greet(dev(yy, z, 1, x))
        pl.semaphore_wait(bar, 1 + NX - 1 + 2 + NY - 1)

    @pl.when(far)
    def _():
        greet(dev(y, z, 1, x))
        for xx in (xp, xm):
            greet(dev(y, z, 0, xx))
        pl.semaphore_wait(bar, NX + 2)

    for i in range(1, NX):
        xt = (x + i) % NX
        remote(act.at[xt], chunk.at[c, x], act_s.at[i], act_r.at[c, i], dev(y, z, 1, xt))

    @pl.when(far)
    def _():
        remote(act.at[x], chunk.at[0, x], act_s.at[0], act_r.at[0, 0], dev(y, z, 1, x))

    @pl.when(near)
    def _():
        pltpu.make_async_copy(act.at[x], chunk.at[1, x], act_r.at[1, 0]).start()
        remote(w, wb.at[1, x], wn_s, wn_r, dev(y, z, 0, x))
        remote(ow, ob.at[1, x], on_s, on_r, dev(y, z, 0, x))

    def gather_send(src, buf, d2, half, ss, rs):
        for q, (first, target) in enumerate(((0, xp), (1, xm))):
            for p in (first, 1 - first):
                rows = pl.ds(p * half, half)
                remote(src.at[rows], buf.at[d2, x, rows], ss, rs.at[d2, q, p], dev(y, z, 0, target))

    def gather_pass(buf, d2, half, q, p, ss, rs, fr_):
        origin = xm if q == 0 else xp
        piece = buf.at[d2, origin, pl.ds(p * half, half)]
        wait(piece, rs.at[d2, q, p])
        if p == q:
            remote(piece, piece, ss, fr_.at[d2, q], dev(y, z, 0, xp if q == 0 else xm))

    def gather_last(buf, d2, half, q, fr_):
        wait(buf.at[d2, xo, pl.ds(q * half, half)], fr_.at[d2, q])

    WH = FEAT * KT // 2
    OH = NOUT * 8 // 2

    def wconv(d2, origin, p):
        def body(kt, carry):
            v = wb[d2, origin, pl.ds(p * WH + kt, FEAT // 2, stride=KT), :]
            hi, lo = split(v)
            lanes = pl.ds(pl.multiple_of(kt * LANE, LANE), LANE)
            at = d2 * FEAT + p * (FEAT // 2)
            whl[origin, pl.ds(at, FEAT // 2), lanes] = hi
            whl[origin, pl.ds(at + 2 * FEAT, FEAT // 2), lanes] = lo
            return carry

        lax.fori_loop(0, KT, body, 0)

    def ysplit(q, n):
        share = (n // 2 + 7) // 8 * 8
        return pl.ds(share, n - share) if q else pl.ds(0, share)

    def core(piece, sem, sent):
        remote(piece, piece, sent, sem, to_far)

    def place(d, s):
        return (NZ - s) % NZ if d else s

    def back(d, s):
        return wrap(z - s, NZ) if d == 0 else wrap(z + s, NZ)

    toward = [dev(y, wrap(z + 1, NZ), 1, x), dev(y, wrap(z - 1, NZ), 1, x)]
    to_yp, to_ym, to_yo = [dev(yy, z, 1, x) for yy in (yp, ym, yo)]
    to_far = dev(y, z, 0, x)

    ONES = pl.ds(0, R1)
    TWOS = pl.ds(R1, R2)

    def cutting(d, s, first, n):
        if s < NZ // 2:
            return pl.ds(first, n)
        share = (n // 2 + 7) // 8 * 8
        return pl.ds(first + share, n - share) if d else pl.ds(first, share)

    def z1piece(u, d, s, t):
        n = R1 // PER
        return g.at[place(d, s - t), y, u // PER, cutting(d, s, u % PER * n, n)]

    def z2piece(u, d, s, t):
        return g.at[place(d, s - t), pl.ds(u % PER * (NY // PER), NY // PER), u // PER, cutting(d, s, R1, R2)]

    def z1(u, d, s):
        remote(z1piece(u, d, s, 1), z1piece(u, d, s, 0), z1_s, r1.at[u, d, s - 1], toward[d])

    def z2(u, d, s):
        remote(z2piece(u, d, s, 1), z2piece(u, d, s, 0), z2_s, r2.at[u, d, s - 1], toward[d])

    def y1(slot, straight):
        piece = g.at[slot, y, :, ONES]
        remote(piece, piece, y_s, ry.at[0, slot], to_yp)
        remote(piece, piece, y_s, ry.at[1, slot], to_ym)
        if straight:
            remote(piece, piece, y_s, rh.at[0, slot], to_yo)
        core(piece, rc.at[slot], c_s)

    def y1pass(slot, straight):
        for q, origin, target in ((0, ym, to_yp), (1, yp, to_ym)):
            wait(g.at[slot, origin, :, ONES], ry.at[q, slot])
            if not straight:
                piece = g.at[slot, origin, :, ysplit(q, R1)]
                remote(piece, piece, h_s, rh.at[q, slot], target)
        core(g.at[slot, ym, :, ONES], rc.at[slot], c_s)
        core(g.at[slot, yp, :, ONES], rc.at[slot], c_s)

    def y1last(slot, straight):
        if straight:
            wait(g.at[slot, yo, :, ONES], rh.at[0, slot])
        else:
            for q in range(2):
                wait(g.at[slot, yo, :, ysplit(q, R1)], rh.at[q, slot])
        core(g.at[slot, yo, :, ONES], rc.at[slot], c_s)

    def spots(s):
        return [(p, s >= STRAIGHT) for p in sorted({place(d, s) for d in range(2)})]

    @pl.when(near)
    def _():
        for cls in range(2):
            for i in range(NX):
                wait(chunk.at[0, 0], act_r.at[cls, i])
        for cls in range(2):
            data = chunk[cls]
            width = TILES * LANE

            def mean(v):
                return jnp.sum(jnp.sum(v, 0, keepdims=True), 2, keepdims=True) / width

            center = mean(data)
            scale = lax.rsqrt(mean(data * data) - center * center + EPS)
            normed = (data - center) * scale
            for t in range(TILES):
                v = normed[t // KT, :, t % KT * LANE : (t % KT + 1) * LANE]
                g[0, y, cls, pl.ds(2 * t, 2), :] = v
            for u in range(PER * cls, PER * cls + PER):
                for d in range(2):
                    z1(u, d, 1)
        own2 = g.at[0, y, :, TWOS]
        for k, target in enumerate((to_yp, to_ym, to_yo)):
            remote(own2, own2, p_s, rp.at[k], target)
        y1(0, False)
        for k, origin in enumerate((ym, yp, yo)):
            wait(g.at[0, origin, :, TWOS], rp.at[k])
        for u in range(STREAMS):
            for d in range(2):
                z2(u, d, 1)
        core(g.at[0, :, :, TWOS], rc.at[0], c2_s)
        last = NZ // 2
        for s in range(1, last + 3):
            if s <= last:
                for u in range(STREAMS):
                    for d in range(2):
                        wait(z1piece(u, d, s, 0), r1.at[u, d, s - 1])
                        if s < last:
                            z1(u, d, s + 1)
                for spot in spots(s):
                    y1(*spot)
            t = s - 1
            if 1 <= t <= last:
                for u in range(STREAMS):
                    for d in range(2):
                        wait(z2piece(u, d, t, 0), r2.at[u, d, t - 1])
                        if t < last:
                            z2(u, d, t + 1)
                for slot, _ in spots(t):
                    core(g.at[slot, :, :, TWOS], rc.at[slot], c2_s)
            if 0 <= s - 1 <= last:
                for spot in spots(s - 1):
                    y1pass(*spot)
            if 0 <= s - 2 <= last:
                for spot in spots(s - 2):
                    y1last(*spot)

    @pl.when(far)
    def _():
        own = pltpu.make_async_copy(w, wb.at[0, x], loc.at[0])
        own.start()
        gather_send(w, wb, 0, WH, w_s, w_r)
        wait(wb.at[1, x], wn_r)
        gather_send(wb.at[1, x], wb, 1, WH, w_s, w_r)
        own.wait()
        for d2 in range(2):
            for p in range(2):
                wconv(d2, x, p)
        for p in range(2):
            for d2 in range(2):
                gather_pass(wb, d2, WH, 0, p, w_s, w_r, wf_r)
                gather_pass(wb, d2, WH, 1, 1 - p, w_s, w_r, wf_r)
            for d2 in range(2):
                wconv(d2, xm, p)
                wconv(d2, xp, 1 - p)
        own = pltpu.make_async_copy(ow, ob.at[0, x], loc.at[1])
        own.start()
        gather_send(ow, ob, 0, OH, o_s, o_r)
        wait(ob.at[1, x], on_r)
        gather_send(ob.at[1, x], ob, 1, OH, o_s, o_r)
        flat_g = g.reshape(NZ * NY * NC * R, LANE)

        def arrive(k, carry):
            away = (k + 1) // 2
            lies = away + (NZ - 2 * away) * (k % 2)
            slot = wrap(z - away + 2 * away * (k % 2), NZ)
            wait(g.at[lies], rc.at[lies])
            rows = pl.ds(pl.multiple_of(slot * 16, 16), 16)
            low = pl.ds(pl.multiple_of(2 * LANE + slot * 16, 16), 16)
            for t in range(TILES):
                v = jnp.concatenate(
                    [flat_g[pl.ds(lies * (NY * NC * R) + 2 * t + b, NY * NC, stride=R), :] for b in range(2)], 0
                )
                hi, lo = split(v)
                lanes = pl.ds(t % KT * LANE, LANE)
                ghl[t // KT, rows, lanes] = hi
                ghl[t // KT, low, lanes] = lo
            return carry

        lax.fori_loop(0, EARLY, arrive, 0)
        for d2 in range(2):
            for q in range(2):
                gather_last(wb, d2, WH, q, wf_r)
                wconv(d2, xo, q)
        own.wait()

        lax.fori_loop(EARLY, NZ, arrive, 0)
        for p in range(2):
            for d2 in range(2):
                gather_pass(ob, d2, OH, 0, p, o_s, o_r, of_r)
                gather_pass(ob, d2, OH, 1, 1 - p, o_s, o_r, of_r)

        acc[...] = jnp.zeros_like(acc)
        turned = (((1,), (1,)), ((), ()))

        def project(k, carry):
            acc[...] += lax.dot_general(whl[k, : 2 * FEAT], ghl[k], turned, preferred_element_type=F32)
            acc[:, :256] += lax.dot_general(
                whl[k, 2 * FEAT :], ghl[k, :256], turned, preferred_element_type=F32
            )
            return carry

        lax.fori_loop(0, NX, project, 0)
        triples = acc[:, :256] + acc[:, 256:]

        msg[...] = jnp.zeros_like(msg)
        for cls in range(2):
            for d2 in range(2):
                for s in range(3):
                    at = d2 * FEAT + s * HEADS
                    msg[cls, pl.ds(2 * s + d2, HEADS, stride=8), :] = triples[
                        at : at + HEADS, cls * LANE : (cls + 1) * LANE
                    ]

        def post(k, carry):
            j = k // NY
            zz = (z // 2 + 4 + (j + 1) // 2 * (1 - 2 * (j % 2))) % NZZ
            yy = (y + 2 + k) % NY
            h = yy * NZZ + zz
            there = yy * NZ + zz * 2
            rows = pl.ds(pl.multiple_of(h * 8, 8), 8)
            dst = rcv.at[pl.ds(pl.multiple_of(me * 8, 8), 8)]
            remote(msg.at[1, rows], dst, a2a_s, a2a_r, (there * 2 + 1, x))

            @pl.when(there != me)
            def _():
                remote(msg.at[0, rows], dst, a2a_s, a2a_r, (there * 2, x))

            @pl.when(there == me)
            def _():
                pltpu.make_async_copy(msg.at[0, rows], dst, a2a_r).start()

            return carry

        lax.fori_loop(0, HEADS, post, 0)

        for d2 in range(2):
            for q in range(2):
                gather_last(ob, d2, OH, q, of_r)

        for d2 in range(2):
            for hq in range(NX):
                for j in range(8):
                    hi, lo = split(ob[d2, hq, pl.ds(j, NOUT, stride=8), :])
                    lanes = pl.ds(hq * LANE, LANE)
                    owhl[j, pl.ds(d2 * NOUT, NOUT), lanes] = hi
                    owhl[j, pl.ds(2 * NOUT + d2 * NOUT, NOUT), lanes] = lo

    @pl.when(near)
    def _():
        drain(z1_s, 4 * (7 * R1 + R1 // 2))
        drain(z2_s, 4 * NY * (7 * R2 + R2 // 2))
        straight = 2 * (NZ // 2 - STRAIGHT) + 1
        drain(y_s, (NZ * 2 + straight) * 2 * R1)
        drain(h_s, (NZ - straight) * 2 * R1)
        drain(c_s, NZ * NY * NC * R1)
        drain(c2_s, NZ * NY * NC * R2)
        drain(p_s, 3 * 2 * R2)

    def norm_rows(v):
        m = jnp.sum(v, 0, keepdims=True) / LANE
        q = jnp.sum(v * v, 0, keepdims=True) / LANE - m * m
        return (v - m) * lax.rsqrt(q + EPS)

    @pl.when(even)
    def _():
        wait(rcv, a2a_r)

        def third(s):
            return jnp.concatenate([rcv[pl.ds(2 * s + d2, 64, stride=8), :] for d2 in range(2)], 0)

        kv[c, pl.ds(0, LANE)] = norm_rows(third(1))
        kv[c, pl.ds(LANE, LANE)] = third(2)
        mine = kv.at[c]
        remote(mine, mine, kv_s, kv_r, dev(y, z, 1 - c, x))
        queries = norm_rows(third(0)) * (LANE ** -0.5)
        wait(kv.at[1 - c], kv_r)
        es = []
        for k in range(2):
            keys = kv[k, pl.ds(0, LANE)].T
            es.append(jnp.exp(jnp.dot(keys, queries, precision=HIGHEST, preferred_element_type=F32)))
        norm = jnp.sum(es[0], 0, keepdims=True) + jnp.sum(es[1], 0, keepdims=True)
        o = sum(
            jnp.dot(kv[k, pl.ds(LANE, LANE)], es[k] / norm, precision=HIGHEST, preferred_element_type=F32)
            for k in range(2)
        )
        for d2 in range(2):
            att[0, y, c, pl.ds(d2, 64, stride=2), :] = o[d2 * 64 : d2 * 64 + 64]

    def lies(d, s):
        return place(d, s) // 2

    def b1piece(u, d, s, t):
        n = A1 // PER
        return att.at[lies(d, s - t), y, u // PER, cutting(d, s, u % PER * n, n)]

    def b2piece(u, d, s, t):
        return att.at[lies(d, s - t), pl.ds(u % PER * (NY // PER), NY // PER), u // PER, cutting(d, s, A1, LANE - A1)]

    def b1(u, d, s):
        remote(b1piece(u, d, s, 1), b1piece(u, d, s, 0), z1_s, r1.at[u, d, s - 1], toward[d])

    def b2(u, d, s):
        remote(b2piece(u, d, s, 1), b2piece(u, d, s, 0), z2_s, r2.at[u, d, s - 1], toward[d])

    FIRST = pl.ds(0, A1)
    SECOND = pl.ds(A1, LANE - A1)

    def v1(slot, straight, own=False):
        piece = att.at[slot, y, :, FIRST]
        remote(piece, piece, y_s, ry.at[0, slot], to_yp)
        remote(piece, piece, y_s, ry.at[1, slot], to_ym)
        if straight:
            remote(piece, piece, y_s, rh.at[0, slot], to_yo)
        if not own:
            core(piece, rc.at[slot], c_s)

    def v1pass(slot, straight):
        for q, origin, target in ((0, ym, to_yp), (1, yp, to_ym)):
            wait(att.at[slot, origin, :, FIRST], ry.at[q, slot])
            if not straight:
                piece = att.at[slot, origin, :, ysplit(q, A1)]
                remote(piece, piece, h_s, rh.at[q, slot], target)
        core(att.at[slot, ym, :, FIRST], rc.at[slot], c_s)
        core(att.at[slot, yp, :, FIRST], rc.at[slot], c_s)

    def v1last(slot, straight):
        if straight:
            wait(att.at[slot, yo, :, FIRST], rh.at[0, slot])
        else:
            for q in range(2):
                wait(att.at[slot, yo, :, ysplit(q, A1)], rh.at[q, slot])
        core(att.at[slot, yo, :, FIRST], rc.at[slot], c_s)

    def places(s):
        return [(p, s >= STRAIGHT) for p in sorted({lies(d, s) for d in range(2)})]

    ACROSS = pl.ds(0, 2 * NOUT)

    @pl.when(far)
    def _():
        acc[ACROSS] = jnp.zeros((2 * NOUT, 4 * LANE), F32)

    def finish(p, slot):
        halves = [split(att[p, :, cls].reshape(NY * LANE, LANE)) for cls in range(2)]
        hi = jnp.concatenate([h for h, _ in halves], 1)
        lo = jnp.concatenate([l for _, l in halves], 1)
        acc[ACROSS] += jnp.dot(
            owhl[slot, : 2 * NOUT], jnp.concatenate([hi, lo], 1), preferred_element_type=F32
        )
        acc[ACROSS, : 2 * LANE] += jnp.dot(owhl[slot, 2 * NOUT :], hi, preferred_element_type=F32)

    def round_of(s, before, earlier):
        last = NZ // 2
        for u in range(STREAMS):
            for d in range(2):
                wait(b1piece(u, d, s, 0), r1.at[u, d, s - 1])
                if s < last:
                    b1(u, d, s + 1)
        for place in places(s):
            v1(*place)
        for place in before:
            v1pass(*place)
        for u in range(STREAMS):
            for d in range(2):
                wait(b2piece(u, d, s, 0), r2.at[u, d, s - 1])
                if s < last:
                    b2(u, d, s + 1)
        for slot, _ in places(s):
            core(att.at[slot, :, :, SECOND], rc.at[slot], c_s)
        for place in earlier:
            v1last(*place)

    def last_of(before, earlier):
        for place in before:
            v1pass(*place)
        for place in earlier:
            v1last(*place)

    @pl.when(near & even)
    def _():
        core(att.at[0, y, 1], rc.at[0], c_s)
        wait(att.at[0, y, 0], b_r)
        for u in range(STREAMS):
            for d in range(2):
                b1(u, d, 1)
        own = att.at[0, y, :, SECOND]
        for k, target in enumerate((to_yp, to_ym, to_yo)):
            remote(own, own, p_s, rp.at[k], target)
        v1(0, False, True)
        for k, origin in enumerate((ym, yp, yo)):
            wait(att.at[0, origin, :, SECOND], rp.at[k])
        for u in range(STREAMS):
            for d in range(2):
                b2(u, d, 1)
        for origin in (ym, yp, yo):
            core(att.at[0, origin, :, SECOND], rc.at[0], c_s)
        round_of(2, places(0), [])
        round_of(4, places(2), places(0))
        round_of(6, places(4), places(2))
        round_of(8, places(6), places(4))
        last_of(places(8), places(6) + places(8))

    @pl.when(near & odd)
    def _():
        round_of(1, [], [])
        round_of(3, places(1), [])
        round_of(5, places(3), places(1))
        round_of(7, places(5), places(3))
        last_of(places(7), places(5) + places(7))

    def from_near(s):
        for d in range(1 if s in (0, NZ // 2) else 2):
            p = lies(d, s)
            if s:
                wait(att.at[p], rc.at[p])
            else:
                drain(rc.at[p], (2 * NY - 1) * LANE)
            finish(p, back(d, s) // 2)

    @pl.when(far & even)
    def _():
        own = att.at[0, y, 0]
        remote(own, own, b_s, b_r, dev(y, z, 1, x))
        for s in (0, 2, 4, 6, 8):
            from_near(s)
        wait(own, b_s)

    @pl.when(far & odd)
    def _():
        for s in (1, 3, 5, 7):
            from_near(s)

    @pl.when(far)
    def _():
        sums = acc[ACROSS, : 2 * LANE] + acc[ACROSS, 2 * LANE :]
        for k in range(2):
            mine = sums[:, k * LANE : (k + 1) * LANE]
            turn[pl.ds(k * LANE, LANE)] = jnp.concatenate([mine, jnp.zeros((LANE - 2 * NOUT, LANE), F32)], 0).T
        for q in range(NX):
            for cls in range(NC):
                mine = turn[pl.ds(q * NC + cls, 2 * NZ, stride=NY * NC), :]
                for cc in range(NC):
                    fs[q, cc, pl.ds(cls * 32, 32), pl.ds(0, NOUT)] = mine[:, cc * NOUT : cc * NOUT + NOUT]
        for dx in (2, 1, 3, 0):
            for cc in range(NC):
                if dx or cc:
                    tx = (x + dx) % NX
                    remote(fs.at[tx, cc], fr.at[x], f_s, f_r.at[dx], dev(y, z, cc, tx))
        fr[x] = fs[x, 0]

    @pl.when(near)
    def _():
        wait(fr.at[0], f_r.at[0])

    for dx in range(1, NX):
        wait(fr.at[0], f_r.at[dx])
    for i in range(NX):
        for cls in range(NC):
            for b in range(2):
                out[i, pl.ds(2 * cls + b, 16, stride=4), :] = fr[i, pl.ds(cls * 32 + b, 16, stride=2), :][:, :NOUT]

    for i in range(1, NX):
        wait(chunk.at[0, 0], act_s.at[i])

    @pl.when(even)
    def _():
        wait(kv.at[0], kv_s)

    @pl.when(far)
    def _():
        wait(chunk.at[0, 0], act_s.at[0])
        drain(w_s, 12 * WH)
        drain(o_s, 12 * OH)
        drain(f_s, 7 * 64)

    @pl.when(far & even)
    def _():
        drain(a2a_s, (2 * HEADS - 1) * 8)

    @pl.when(far & odd)
    def _():
        drain(a2a_s, 2 * HEADS * 8)

    @pl.when(near)
    def _():
        drain(wn_s, 2 * WH)
        drain(on_s, 2 * OH)

    @pl.when(near & even)
    def _():
        drain(z1_s, 2 * NC * 4 * A1)
        drain(z2_s, 2 * NC * 4 * NY * (LANE - A1))
        drain(y_s, (NZZ * 2 + 1) * 2 * A1)
        drain(h_s, (NZZ - 1) * 2 * A1)
        drain(c_s, NZZ * NY * NC * LANE - LANE)
        drain(p_s, 3 * 2 * (LANE - A1))

    @pl.when(near & odd)
    def _():
        drain(z1_s, NC * 7 * A1)
        drain(z2_s, NC * 7 * NY * (LANE - A1))
        drain(y_s, (NZZ * 2 + 2) * 2 * A1)
        drain(h_s, (NZZ - 2) * 2 * A1)
        drain(c_s, NZZ * NY * NC * LANE)


def shards(activations, input_weight, output_weight):
    w = input_weight.reshape(FEAT * KT, LANE)
    ow = output_weight.reshape(NOUT * 8, LANE)
    dma = pltpu.SemaphoreType.DMA
    vm = pltpu.VMEM
    scratch = [
        vm((NC, NX, 2, KT * LANE), F32),
        vm((NZ, NY, NC, R, LANE), F32),
        vm((NC, NX, FEAT * KT, LANE), F32),
        vm((NX, 4 * FEAT, KT * LANE), BF16),
        vm((NX, 4 * LANE, KT * LANE), BF16),
        vm((NC, NX, NOUT * 8, LANE), F32),
        vm((NZZ, 4 * NOUT, NY * LANE), BF16),
        vm((NC, HEADS * 8, LANE), F32),
        vm((NY * NZ * 8, LANE), F32),
        vm((NC, 2 * LANE, LANE), F32),
        vm((NZZ, NY, NC, LANE, LANE), F32),
        vm((NX, NC, 64, LANE), F32),
        vm((NX, 64, LANE), F32),
        vm((2 * LANE, LANE), F32),
        vm((2 * FEAT, 4 * LANE), F32),
        dma((NX,)), dma((NC, NX)),
        dma, dma((2, 2, 2)), dma((2, 2)), dma, dma,
        dma, dma((2, 2, 2)), dma((2, 2)), dma, dma,
        dma, dma, dma, dma, dma, dma, dma,
        dma((STREAMS, 2, 8)), dma((STREAMS, 2, 8)),
        dma((2, NZ)), dma((2, NZ)), dma((3,)),
        dma((NZ,)),
        dma, dma, dma, dma, dma, dma,
        dma, dma((NX,)),
        dma((2,)),
    ]
    return pl.pallas_call(
        kernel,
        out_shape=jax.ShapeDtypeStruct((NX, 64, NOUT), F32),
        in_specs=[
            pl.BlockSpec(memory_space=pl.ANY),
            pl.BlockSpec(memory_space=pl.ANY),
            pl.BlockSpec(memory_space=pl.ANY),
        ],
        out_specs=pl.BlockSpec(memory_space=pltpu.VMEM),
        scratch_shapes=scratch,
        compiler_params=pltpu.CompilerParams(
            collective_id=0, has_side_effects=True, vmem_limit_bytes=60 * 1024 * 1024
        ),
    )(activations, w, ow)


def solution(mesh):
    return jax.shard_map(
        shards,
        mesh=mesh,
        in_specs=(P(None, "row", "col"), P(None, None, "row", "col"), P("row", "col", None)),
        out_specs=P(None, "col", "row"),
        check_vma=False,
    )
```
